512 devices in a mesh: seq: 32 (over y_hi, x, core), dp: 16 (over z, y_lo).
Axes of the slice: x: 4, y: 8 (y_hi: 4, y_lo: 2; y = y_hi * 2 + y_lo), z: 8, core: 2. Of those that a mesh axis runs over, the one named last changes fastest.
Arguments:
- hidden_in: bfloat16 [16, 4096, 8192], P('dp', 'seq'), may hold values from -6 to 6
- queries: bfloat16 [16, 4096, 4096], P('dp', 'seq'), may hold values from -512 to 512
- keys: bfloat16 [16, 4096, 1024], P('dp', 'seq'), may hold values from -4 to 4
- values: bfloat16 [16, 4096, 1024], P('dp', 'seq'), may hold values from -6 to 6
- out_grad: bfloat16 [16, 4096, 4096], P('dp', 'seq'), may hold values from -6 to 6
- doc_ids: int32 [16, 4096], P('dp', 'seq'), may hold values from 0 to 63, never falling along the last dimension, each value on 1 to 128 neighbouring positions
- projection: bfloat16 [8192, 256], P('dp'), may hold values from -0.0625 to 0.0625
- mom1_q: float32 [256, 4096], P('dp', 'seq'), may hold values from -18 to 18
- mom2_q: float32 [256, 4096], P('dp', 'seq'), may hold values from 4 to 400
- mom1_kv: float32 [2, 256, 1024], P(None, 'dp', 'seq'), may hold values from -18 to 18
- mom2_kv: float32 [2, 256, 1024], P(None, 'dp', 'seq'), may hold values from 4 to 400
Outputs:
- new_mom1_q: float32 [256, 4096], P('dp', 'seq')
- new_mom2_q: float32 [256, 4096], P('dp', 'seq')
- update_q: float32 [256, 4096], P('dp', 'seq')
- new_mom1_kv: float32 [2, 256, 1024], P(None, 'dp', 'seq')
- new_mom2_kv: float32 [2, 256, 1024], P(None, 'dp', 'seq')
- update_kv: float32 [2, 256, 1024], P(None, 'dp', 'seq')
The draws below stay inside these ranges and needn't reach their ends.
Inputs may be any that keep to these rules, and one draw needn't show every extreme that they name: `doc_ids`: document ids never fall along a replica's positions, and one document holds at most 128 positions.
All inputs are finite; a program needn't handle non-finite values.
Results may differ from the reference program's by a relative error of at most 0.019.
Values may be sent and summed in bfloat16 or wider, within the bound.
A program may use at most 128 MiB of HBM per device.

```python
import math
import jax
import jax.numpy as jnp
import numpy as np
from jax import lax

D = 8192
H = 32
KVH = 8
HD = 128
RANK = 256
GROUP = 4
ADAM_STEP = 100
SEQ_TOKENS = 4096
SEQ_LEN = 4096
DOC_MOST = 128
REPLICAS = 16
DOCS = 64


def key_basis(key):
    normal_keys = jax.random.normal(jax.random.fold_in(key, 101), (REPLICAS, SEQ_TOKENS, KVH, HD), jnp.float32)
    return jnp.clip(normal_keys, -4.0, 4.0)


def draw_keys(key, part):
    basis = key_basis(key)
    return basis.reshape(REPLICAS, SEQ_TOKENS, KVH * HD).astype(jnp.bfloat16)


def draw_queries(key, part):
    drawn_rows = jax.random.normal(jax.random.fold_in(key, 102), (REPLICAS, SEQ_TOKENS, H, HD), jnp.float32)
    drawn_rows = jnp.clip(drawn_rows, -6.0, 6.0)
    return drawn_rows.reshape(REPLICAS, SEQ_TOKENS, H * HD).astype(jnp.bfloat16)


def level_of(stream_key, shape, split, smallest, largest):
    def one(axis_at, parts):
        heights = jax.random.uniform(jax.random.fold_in(jax.random.fold_in(stream_key, 6), axis_at), (parts,), jnp.float32, smallest / len(split), largest / len(split))
        return jnp.repeat(jnp.exp(heights), shape[axis_at] // parts).reshape((-1,) + (1,) * (len(shape) - axis_at - 1))

    level = one(*split[0])
    for cut in split[1:]:
        level = level * one(*cut)
    return level


def length_profile(count, total, limit, slope):
    weights = [(1 << 20) // math.isqrt(standing ** slope) + 1 for standing in range(2, count + 1)]
    surplus, counts = total - limit - (count - 1), [1] * (count - 1)
    while surplus > 0:
        movable = [i for i in range(count - 1) if counts[i] < limit]
        whole, left = sum([weights[i] for i in movable]), surplus
        for i in movable:
            more = min(limit - counts[i], max(1, left * weights[i] // whole), surplus)
            counts[i] = counts[i] + more
            surplus = surplus - more
    return np.array([limit] + counts)


def ragged_sizes(rng, amount, total, limit, skew):
    if amount == 2:
        one = jax.random.randint(rng, (), max(1, total - limit), min(limit, total - 1) + 1)
        return jnp.stack([one, total - one])
    sizes = jnp.asarray(length_profile(amount, total, limit, skew), jnp.int32)
    twos = (amount - 1) // 2
    donor, sink = sizes[1:1 + 2 * twos:2], sizes[2:2 + 2 * twos:2]
    margin = jnp.minimum(donor - 1, limit - sink)
    shifted = jax.random.randint(jax.random.fold_in(rng, 1), (twos,), 0, 1 << 20) % (margin + 1)
    sizes = sizes.at[1:1 + 2 * twos:2].set(donor - shifted).at[2:2 + 2 * twos:2].set(sink + shifted)
    return sizes[jax.random.permutation(jax.random.fold_in(rng, 2), amount)]


def noise(stream_key, dims, width, bound, shards=(), dtype=jnp.bfloat16):
    gain = level_of(stream_key, dims, shards, -0.22, 0.18) if shards else 1.0
    drawn = jax.random.normal(stream_key, dims, jnp.float32) * width * gain
    return jnp.minimum(jnp.maximum(drawn, -bound), bound).astype(dtype)


def setup_inputs(seed: int = 0) -> dict:
    streams_of = jax.random.split(jax.random.key(seed), 12)
    return {
        "hidden_in": noise(streams_of[0], (REPLICAS, SEQ_TOKENS, D), 1.0, 6.0, ((0, 16), (1, 32))),
        "queries": draw_queries(jax.random.fold_in(streams_of[11], 71), 0),
        "keys": draw_keys(jax.random.fold_in(streams_of[11], 71), 0),
        "values": noise(streams_of[3], (REPLICAS, SEQ_TOKENS, KVH * HD), 1.0, 6.0, ((0, 16), (1, 32))),
        "out_grad": noise(streams_of[4], (REPLICAS, SEQ_TOKENS, H * HD), 1.0, 6.0, ((0, 16), (1, 32))),
        "doc_ids": jax.vmap(lambda own: jnp.searchsorted(jnp.cumsum(ragged_sizes(own, DOCS, SEQ_TOKENS, DOC_MOST, 1)), jnp.arange(SEQ_TOKENS), side="right"))(jax.random.split(streams_of[5], REPLICAS)).reshape((REPLICAS, SEQ_TOKENS)).astype(jnp.int32),
        "projection": noise(streams_of[6], (D, RANK), D ** -0.5, 0.0625, ((0, 16),)),
        "mom1_q": noise(streams_of[7], (RANK, H * HD), 3.0, 18.0, ((0, 16), (1, 32)), jnp.float32),
        "mom2_q": jnp.clip(jnp.exp(math.log(400.0) - 4.6051702 * jax.random.uniform(streams_of[8], (RANK, H * HD), jnp.float32) ** level_of(streams_of[8], (RANK, H * HD), ((0, 16), (1, 32)), -0.2, 0.2)), 4.0, 400.0),
        "mom1_kv": noise(streams_of[9], (2, RANK, KVH * HD), 3.0, 18.0, ((1, 16), (2, 32)), jnp.float32),
        "mom2_kv": jnp.clip(jnp.exp(math.log(400.0) - 4.6051702 * jax.random.uniform(streams_of[10], (2, RANK, KVH * HD), jnp.float32) ** level_of(streams_of[10], (2, RANK, KVH * HD), ((1, 16), (2, 32)), -0.2, 0.2)), 4.0, 400.0),
    }


beta_first = 0.9
beta_second = 0.999
adam_epsilon = 1e-08

def sequence_grads(seq_items):
    query, keyset, valueset, outgrad, documents = seq_items
    score_scale = 1.0 / HD ** 0.5
    query_wide = query.astype(jnp.float32)
    key_wide = keyset.astype(jnp.float32)
    value_wide = valueset.astype(jnp.float32)
    grad_wide = outgrad.astype(jnp.float32)
    scores = jnp.einsum('qd,kd->qk', query_wide, key_wide) * score_scale
    places = jnp.arange(SEQ_LEN)
    visible = (places[None, :] <= places[:, None]) & (documents[None, :] == documents[:, None])
    masked = jnp.where(visible, scores, -jnp.inf)
    row_peak = lax.optimization_barrier(jnp.max(masked, axis=1, keepdims=True))
    weights = jnp.exp(masked - row_peak)
    attention = weights / lax.optimization_barrier(jnp.sum(weights, axis=1, keepdims=True))
    attention_low = attention.astype(jnp.bfloat16)
    attention_back = attention_low.astype(jnp.float32)
    output = jnp.einsum('qk,kd->qd', attention_back, value_wide)
    row_delta = lax.optimization_barrier(jnp.sum(grad_wide * output, axis=1, keepdims=True))
    grad_attention = jnp.einsum('qd,kd->qk', grad_wide, value_wide)
    grad_scores = (attention * (grad_attention - row_delta)).astype(jnp.bfloat16)
    scores_back = grad_scores.astype(jnp.float32)
    grad_query = (jnp.einsum('qk,kd->qd', scores_back, key_wide) * score_scale).astype(jnp.bfloat16)
    grad_key = (jnp.einsum('qk,qd->kd', scores_back, query_wide) * score_scale).astype(jnp.bfloat16)
    grad_value = jnp.einsum('qk,qd->kd', attention_back, grad_wide).astype(jnp.bfloat16)
    return (grad_query, grad_key, grad_value)

def adam_update(first_moment, second_moment, gradient):
    first_new = beta_first * first_moment + (1.0 - beta_first) * gradient
    second_new = beta_second * second_moment + (1.0 - beta_second) * gradient * gradient
    corrected_first = first_new / (1.0 - beta_first ** ADAM_STEP)
    corrected_second = second_new / (1.0 - beta_second ** ADAM_STEP)
    return (first_new, second_new, corrected_first / (jnp.sqrt(corrected_second) + adam_epsilon))

def reference(hidden_in, queries, keys, values, out_grad, doc_ids, projection, mom1_q, mom2_q, mom1_kv, mom2_kv):
    seq_count = SEQ_TOKENS // SEQ_LEN

    def by_heads(block_rows, count):
        return block_rows.reshape(SEQ_TOKENS, count, HD).transpose(1, 0, 2).reshape(count, seq_count, SEQ_LEN, HD)

    def replica_terms(running, replica_items):
        hidden_rows, query_rows, key_rows, value_rows, grad_rows, documents = replica_items
        lowrank = jnp.dot(hidden_rows, projection, preferred_element_type=jnp.float32).astype(jnp.bfloat16)
        key_full = jnp.repeat(key_rows.reshape(SEQ_TOKENS, KVH, HD), GROUP, axis=1).reshape(SEQ_TOKENS, H * HD)
        value_full = jnp.repeat(value_rows.reshape(SEQ_TOKENS, KVH, HD), GROUP, axis=1).reshape(SEQ_TOKENS, H * HD)
        doc_blocks = documents.reshape(seq_count, SEQ_LEN)

        def head_terms(head_items):
            query_head, key_head, value_head, grad_head = head_items
            return lax.map(sequence_grads, (query_head, key_head, value_head, grad_head, doc_blocks))
        grad_q, grad_k, grad_v = lax.map(head_terms, (by_heads(query_rows, H), by_heads(key_full, H), by_heads(value_full, H), by_heads(grad_rows, H)))
        lowrank_wide = lowrank.astype(jnp.float32)

        def project_heads(grads):
            return jnp.einsum('tr,htd->rhd', lowrank_wide, grads.reshape(H, SEQ_TOKENS, HD).astype(jnp.float32))
        term_query = project_heads(grad_q).reshape(RANK, H * HD)
        term_key = project_heads(grad_k).reshape(RANK, KVH, GROUP, HD).sum(axis=2).reshape(RANK, KVH * HD)
        term_value = project_heads(grad_v).reshape(RANK, KVH, GROUP, HD).sum(axis=2).reshape(RANK, KVH * HD)
        return ((running[0] + term_query, running[1] + jnp.stack([term_key, term_value])), None)
    start_state = (jnp.zeros((RANK, H * HD), jnp.float32), jnp.zeros((2, RANK, KVH * HD), jnp.float32))
    totals, unused = lax.scan(replica_terms, start_state, (hidden_in, queries, keys, values, out_grad, doc_ids))
    proj_query, proj_pair = totals
    first_query, second_query, update_query = adam_update(mom1_q, mom2_q, proj_query)
    first_pair, second_pair, update_pair = adam_update(mom1_kv, mom2_kv, proj_pair)
    return (first_query, second_query, update_query, first_pair, second_pair, update_pair)
```

```python
import jax
import jax.numpy as jnp
from jax import lax
from jax.experimental import pallas as pl
from jax.experimental.pallas import tpu as pltpu
from jax.sharding import PartitionSpec as P

H = 32
KVH = 8
HD = 128
RANK = 256
TOK = 128
DEPTH = 8192
ADAM_STEP = 100

beta_first = 0.9
beta_second = 0.999
adam_epsilon = 1e-08

MESH = pl.DeviceIdType.MESH
SIZES = {"core": 2, "x": 4, "y": 8, "z": 8}
BF = jnp.bfloat16
F32 = jnp.float32
QCOLS = H * HD
KCOLS = KVH * HD
PIECES = 4
PIECE = KCOLS // PIECES
BLOCK = 512
HALF = 256
QUARTER = 128


def rem(a, n):
    return lax.rem(a, n)


def here():
    s = lax.axis_index("seq")
    d = lax.axis_index("dp")
    return {
        "core": rem(s, 2),
        "x": rem(s // 2, 4),
        "y": (s // 8) * 2 + rem(d, 2),
        "z": d // 2,
    }


def device(c):
    return {
        "seq": (c["y"] // 2) * 8 + c["x"] * 2 + c["core"],
        "dp": c["z"] * 2 + rem(c["y"], 2),
    }


def moved(c, axis, k):
    n = SIZES[axis]
    out = dict(c)
    out[axis] = rem(c[axis] + (k % n), n)
    return out


def dot_rows(a, b):
    return lax.dot_general(a, b, (((1,), (1,)), ((), ())), preferred_element_type=F32)


def dot_plain(a, b):
    return lax.dot_general(a, b, (((1,), (0,)), ((), ())), preferred_element_type=F32)


def dot_first(a, b):
    return lax.dot_general(a, b, (((0,), (0,)), ((), ())), preferred_element_type=F32)


def kernel(
    hid_in, q_in, k_in, v_in, g_in, doc_in, proj_in,
    outq_ref, outkv_ref,
    hid, q, g, kw, vw, docs, bias, pg, dq, dk, dv, lr, dup, perm,
    zq, rq, xq, xr, yq, yr, wq, wr,
    zk, rk, ck, cr, xk, xkr, yk, ykr, kv_sum,
    load_sem,
    halo_send, halo_recv,
    gz_send, gz_recv, gy_send, gy_recv, gc_send, gc_recv,
    rc_send, rc_recv, qx_send, qx_recv, qy_send, qy_recv, qz_send, qz_recv,
    kz_send, kz_recv, kx_send, kx_recv, ky_send, ky_recv,
):
    c = here()
    s = lax.axis_index("seq")
    d = lax.axis_index("dp")
    core, x, y, z = c["core"], c["x"], c["y"], c["z"]
    y_lo = rem(y, 2)
    nxt = {"seq": rem(s + 1, 32), "dp": d}
    prv = {"seq": rem(s + 31, 32), "dp": d}
    sibling = device(moved(c, "core", 1))

    def zstep(k):
        return rem(z + jnp.where(core == 0, k + 8, 8 - k), 8)

    def zdev(k):
        n = dict(c)
        n["z"] = zstep(k)
        return device(n)

    barrier = pltpu.get_barrier_semaphore()
    peers = [nxt, prv, sibling]
    for axis in ("x", "y", "z"):
        for k in range(1, SIZES[axis]):
            peers.append(device(moved(c, axis, k)))
    for p in peers:
        pl.semaphore_signal(barrier, inc=1, device_id=p, device_id_type=MESH)

    loads = [
        pltpu.make_async_copy(doc_in, docs.at[0], load_sem.at[0]),
        pltpu.make_async_copy(k_in, kw.at[pl.ds(TOK, TOK)], load_sem.at[1]),
        pltpu.make_async_copy(v_in, vw.at[pl.ds(TOK, TOK)], load_sem.at[2]),
        pltpu.make_async_copy(q_in, q, load_sem.at[3]),
        pltpu.make_async_copy(g_in, g, load_sem.at[4]),
        pltpu.make_async_copy(
            proj_in, pg.at[pl.ds(pl.multiple_of(d * BLOCK, BLOCK), BLOCK)], load_sem.at[5]
        ),
        pltpu.make_async_copy(hid_in, hid, load_sem.at[6]),
    ]
    for cp in loads:
        cp.start()

    pl.semaphore_wait(barrier, len(peers))

    def remote(src, dst, send, recv, to):
        return pltpu.make_async_remote_copy(
            src_ref=src, dst_ref=dst, send_sem=send, recv_sem=recv, device_id=to, device_id_type=MESH
        )

    sent = []

    def go(cp):
        cp.start()
        sent.append(cp)
        return cp

    def prow(w, b, h, u=None):
        if u is None:
            return pg.at[pl.ds(pl.multiple_of((w * 2 + b) * BLOCK + h * HALF, HALF), HALF)]
        return pg.at[pl.ds(pl.multiple_of((w * 2 + b) * BLOCK + h * HALF + u * QUARTER, QUARTER), QUARTER)]

    own_half = proj_in.at[pl.ds(pl.multiple_of(core * HALF, HALF), HALF)]

    def own_quarter(u):
        return proj_in.at[pl.ds(pl.multiple_of(core * HALF + u * QUARTER, QUARTER), QUARTER)]

    zf, zb = zdev(1), zdev(-1)
    yu, yd = device(moved(c, "y", 1)), device(moved(c, "y", -1))
    go(remote(own_half, prow(z, y_lo, core), gz_send.at[0], gz_recv.at[0], zf))
    go(remote(own_half, prow(z, y_lo, core), gz_send.at[4], gz_recv.at[4], zb))
    halo = []
    for i in range(PIECES):
        cols = pl.ds(i * PIECE, PIECE)
        a = remote(k_in.at[:, cols], kw.at[pl.ds(0, TOK), cols], halo_send.at[i], halo_recv.at[i], nxt)
        b = remote(
            v_in.at[:, cols], vw.at[pl.ds(0, TOK), cols], halo_send.at[PIECES + i], halo_recv.at[PIECES + i], nxt
        )
        if i == 0:
            loads[0].wait()
            go(remote(docs.at[0], docs.at[1], halo_send.at[2 * PIECES], halo_recv.at[2 * PIECES], nxt))
        go(a)
        go(b)
        halo.append((a, b))

    def y_sends(slot, srcs, w):
        go(remote(srcs[0], prow(w, y_lo, core, 0), gy_send.at[2 * slot], gy_recv.at[2 * slot], yu))
        go(remote(srcs[1], prow(w, y_lo, core, 1), gy_send.at[2 * slot + 1], gy_recv.at[2 * slot + 1], yd))

    y_sends(0, [own_quarter(0), own_quarter(1)], z)

    def core_send(slot, w, b):
        ref = prow(w, b, core)
        go(remote(ref, ref, gc_send.at[slot], gc_recv.at[slot], sibling))

    def z_arrival(slot, k):
        w = zstep(-k)
        ref = prow(w, y_lo, core)
        last = slot in (3, 6)
        remote(ref, ref, gz_send.at[slot], gz_recv.at[slot], zf).wait_recv()
        if not last:
            go(remote(ref, ref, gz_send.at[slot + 1], gz_recv.at[slot + 1], zf if slot < 4 else zb))
        y_sends(slot + 1, [prow(w, y_lo, core, 0), prow(w, y_lo, core, 1)], w)
        core_send(slot, w, y_lo)

    def y_arrival(slot, k):
        w = zstep(-k)
        for u, frm in ((0, yu), (1, yd)):
            ref = prow(w, 1 - y_lo, core, u)
            remote(ref, ref, gy_send.at[2 * slot + u], gy_recv.at[2 * slot + u], frm).wait_recv()
        core_send(7 + slot, w, 1 - y_lo)

    def core_arrival(slot, k, b):
        ref = prow(zstep(k), b, 1 - core)
        remote(ref, ref, gc_send.at[slot], gc_recv.at[slot], sibling).wait_recv()

    z_order = [(0, 1), (4, -1), (1, 2), (5, -2), (2, 3), (6, -3), (3, 4)]
    y_order = [(0, 0)] + [(slot + 1, k) for slot, k in z_order]

    remote(docs.at[0], docs.at[1], halo_send.at[2 * PIECES], halo_recv.at[2 * PIECES], nxt).wait_recv()
    mine = jnp.broadcast_to(docs[0].astype(F32), (TOK, TOK))
    before = jnp.broadcast_to(docs[1].astype(F32), (TOK, TOK))
    before = jnp.where(s == 0, -1.0, before)
    rows = jnp.transpose(mine)
    causal = lax.broadcasted_iota(jnp.int32, (TOK, TOK), 1) <= lax.broadcasted_iota(jnp.int32, (TOK, TOK), 0)
    bias[:, TOK:] = jnp.where(causal & (mine == rows), 0.0, -jnp.inf)
    bias[:, :TOK] = jnp.where(before == rows, 0.0, -jnp.inf)

    ri = lax.broadcasted_iota(jnp.int32, (RANK, 512), 0)
    ci = lax.broadcasted_iota(jnp.int32, (RANK, 512), 1)
    want = ((ci & 127) >> 3) * 16 + (ci >> 7) * 4 + (ci & 3)
    dup[...] = jnp.where(ri == want, 1.0, 0.0).astype(BF)
    ri = lax.broadcasted_iota(jnp.int32, (512, 512), 0)
    ci = lax.broadcasted_iota(jnp.int32, (512, 512), 1)
    want = ((ci & 127) >> 5) * 128 + (ci >> 7) * 32 + (ci & 31)
    perm[...] = jnp.where(ri == want, 1.0, 0.0).astype(BF)

    score_scale = 1.0 / HD**0.5

    def attend(gi, carry):
        wide = pl.multiple_of(gi * 512, 512)
        thin = pl.multiple_of(gi * HD, HD)
        qh = [q[:, pl.ds(wide + j * HD, HD)] for j in range(4)]
        gh = [g[:, pl.ds(wide + j * HD, HD)] for j in range(4)]
        q4 = jnp.concatenate(qh, axis=0)
        g4 = jnp.concatenate(gh, axis=0)
        kwin = kw[:, pl.ds(thin, HD)]
        vwin = vw[:, pl.ds(thin, HD)]
        sc = dot_rows(q4, kwin).reshape(4, TOK, 256) * score_scale + bias[...][None]
        sc = sc.reshape(512, 256)
        peak = jnp.max(sc, axis=1, keepdims=True)
        e = jnp.exp(sc - peak)
        att = e * (1.0 / jnp.sum(e, axis=1, keepdims=True))
        low = att.astype(BF)
        da = dot_rows(g4, vwin)
        delta = jnp.sum(low.astype(F32) * da, axis=1, keepdims=True)
        ds = (att * (da - delta)).astype(BF)
        dqv = (dot_plain(ds, kwin) * score_scale).astype(BF)
        for j in range(4):
            dq[:, pl.ds(wide + j * HD, HD)] = dqv[j * TOK : (j + 1) * TOK]
        dk[:, pl.ds(thin, HD)] = (dot_first(ds, q4) * score_scale).astype(BF)
        dv[:, pl.ds(thin, HD)] = dot_first(low, g4).astype(BF)
        return carry

    def halo_wait(i):
        for cp in halo[i]:
            cp.wait_recv()

    for cp in loads[1:5]:
        cp.wait()
    halo_wait(0)
    lax.fori_loop(0, 2, attend, 0)
    z_arrival(*z_order[0])
    z_arrival(*z_order[1])
    y_arrival(*y_order[0])
    halo_wait(1)
    lax.fori_loop(2, 4, attend, 0)
    z_arrival(*z_order[2])
    z_arrival(*z_order[3])
    y_arrival(*y_order[1])
    y_arrival(*y_order[2])
    halo_wait(2)
    lax.fori_loop(4, 6, attend, 0)
    z_arrival(*z_order[4])
    z_arrival(*z_order[5])
    y_arrival(*y_order[3])
    y_arrival(*y_order[4])
    halo_wait(3)
    lax.fori_loop(6, 8, attend, 0)
    z_arrival(*z_order[6])
    for i in range(5, 8):
        y_arrival(*y_order[i])
    for slot, k in z_order:
        core_arrival(slot, k, y_lo)
    for slot, k in y_order:
        core_arrival(7 + slot, k, 1 - y_lo)
    loads[5].wait()
    loads[6].wait()

    lr[pl.ds(TOK, TOK)] = dot_plain(hid[...], pg[...]).astype(BF)
    lr_copy = go(
        remote(lr.at[pl.ds(TOK, TOK)], lr.at[pl.ds(0, TOK)], halo_send.at[2 * PIECES + 1], halo_recv.at[2 * PIECES + 1], nxt)
    )
    own_lr = lr[pl.ds(TOK, TOK)]

    def project(gi):
        part = dot_first(own_lr, dq[:, pl.ds(pl.multiple_of(gi * 512, 512), 512)]).astype(BF)
        for j in range(4):
            piece = part[:, j * HD : (j + 1) * HD].reshape(8, 2, 16, HD)
            at_x = rem(2 * gi + j // 2, 4)
            for lo in range(2):
                zq[j % 2, at_x, (gi // 2) * 2 + lo] = piece[:, lo]

    def project_even(i, carry):
        project(2 * i)
        return carry

    def project_odd(i, carry):
        project(2 * i + 1)
        return carry

    lax.fori_loop(0, 4, project_even, 0)
    qc = [go(remote(zq.at[1 - core, pl.ds(0, 2)], rq.at[pl.ds(0, 2)], rc_send.at[0], rc_recv.at[0], sibling))]
    lax.fori_loop(0, 4, project_odd, 0)
    qc.append(go(remote(zq.at[1 - core, pl.ds(2, 2)], rq.at[pl.ds(2, 2)], rc_send.at[1], rc_recv.at[1], sibling)))

    lr_copy.wait_recv()
    spread = dot_plain(lr[...], dup[...]).astype(BF)
    kind = (lax.broadcasted_iota(jnp.int32, (256, 512), 1) >> 2) & 1
    left_k = jnp.where(kind == 0, spread, jnp.zeros_like(spread))
    left_v = jnp.where(kind == 1, spread, jnp.zeros_like(spread))
    for a in range(KVH):
        cols = slice(a * HD, (a + 1) * HD)
        both = (dot_first(left_k, dk[:, cols]) + dot_first(left_v, dv[:, cols])).astype(BF)
        wide = jnp.concatenate([both[i * 128 : (i + 1) * 128] for i in range(4)], axis=1)
        wide = dot_plain(wide, perm[...]).astype(BF)
        for b in range(4):
            zk[b % 2, :, (a % 2) * 2 + b // 2, a // 2] = wide[:, b * HD : (b + 1) * HD].reshape(8, 16, HD)
    kc = go(remote(zk.at[1 - core], rk, rc_send.at[2], rc_recv.at[2], sibling))

    for cp in qc:
        cp.wait_recv()
    qx = []
    for k in (2, 1, 3, 0):
        at = rem(x + k, 4)
        xq[at] = (zq[core, at].astype(F32) + rq[at].astype(F32)).astype(BF)
        if k:
            qx.append(go(remote(xq.at[at], xr.at[k - 1], qx_send.at[k - 1], qx_recv.at[k - 1], device(moved(c, "x", k)))))
    kc.wait_recv()
    kz = []
    for k in (4, 3, 5, 2, 6, 1, 7, 0):
        at = rem(z + k, 8)
        ck[at] = (zk[core, at].astype(F32) + rk[at].astype(F32)).astype(BF)
        if k:
            kz.append(go(remote(ck.at[at], cr.at[k - 1], kz_send.at[k - 1], kz_recv.at[k - 1], device(moved(c, "z", k)))))

    for cp in qx:
        cp.wait_recv()
    qy = []
    for k in (4, 3, 5, 2, 6, 1, 7, 0):
        at = rem(y + k, 8)
        tot = xq[x, at].astype(F32)
        for i in range(3):
            tot = tot + xr[i, at].astype(F32)
        yq[at] = tot.astype(BF)
        if k:
            qy.append(go(remote(yq.at[at], yr.at[k - 1], qy_send.at[k - 1], qy_recv.at[k - 1], device(moved(c, "y", k)))))
    for cp in kz:
        cp.wait_recv()
    kx = []
    for k in (2, 1, 3, 0):
        at = rem(x + k, 4)
        tot = ck[z, at].astype(F32)
        for i in range(7):
            tot = tot + cr[i, at].astype(F32)
        xk[at] = tot.astype(BF)
        if k:
            kx.append(go(remote(xk.at[at], xkr.at[k - 1], kx_send.at[k - 1], kx_recv.at[k - 1], device(moved(c, "x", k)))))
    for cp in qy:
        cp.wait_recv()
    tot = yq[y].astype(F32)
    for i in range(7):
        tot = tot + yr[i].astype(F32)
    wq[...] = tot.astype(BF)
    qz = []
    for k in (4, 3, 5, 2, 6, 1, 7):
        at = rem(z + k, 8)
        qz.append(go(remote(wq.at[at], wr.at[k - 1], qz_send.at[k - 1], qz_recv.at[k - 1], device(moved(c, "z", k)))))
    for cp in kx:
        cp.wait_recv()
    tot = xk[x].astype(F32)
    for i in range(3):
        tot = tot + xkr[i].astype(F32)
    yk[...] = tot.astype(BF)
    ky = []
    for k in (4, 3, 5, 2, 6, 1, 7):
        to = moved(c, "y", k)
        ky.append(go(remote(yk.at[to["y"] // 2], ykr.at[k - 1], ky_send.at[k - 1], ky_recv.at[k - 1], device(to))))
    for cp in qz:
        cp.wait_recv()
    tot = wq[z].astype(F32)
    for i in range(7):
        tot = tot + wr[i].astype(F32)
    outq_ref[...] = tot
    for cp in ky:
        cp.wait_recv()
    tot = yk[y // 2].astype(F32)
    for i in range(7):
        tot = tot + ykr[i].astype(F32)
    kv_sum[...] = tot
    outkv_ref[...] = kv_sum[pl.ds(pl.multiple_of(y_lo * 8, 8), 8)]
    for cp in sent:
        cp.wait_send()


def reduced(hid, q, k, v, g, docs, proj):
    any_spec = pl.BlockSpec(memory_space=pl.ANY)
    vmem = pl.BlockSpec(memory_space=pltpu.VMEM)
    dma = pltpu.SemaphoreType.DMA
    halos = 2 * PIECES + 2
    scratch = [
        pltpu.VMEM((TOK, DEPTH), BF),
        pltpu.VMEM((TOK, QCOLS), BF),
        pltpu.VMEM((TOK, QCOLS), BF),
        pltpu.VMEM((2 * TOK, KCOLS), BF),
        pltpu.VMEM((2 * TOK, KCOLS), BF),
        pltpu.VMEM((2, 1, TOK), jnp.int32),
        pltpu.VMEM((TOK, 2 * TOK), F32),
        pltpu.VMEM((DEPTH, RANK), BF),
        pltpu.VMEM((TOK, QCOLS), BF),
        pltpu.VMEM((2 * TOK, KCOLS), BF),
        pltpu.VMEM((2 * TOK, KCOLS), BF),
        pltpu.VMEM((2 * TOK, RANK), BF),
        pltpu.VMEM((RANK, 512), BF),
        pltpu.VMEM((512, 512), BF),
        pltpu.VMEM((2, 4, 8, 8, 16, HD), BF),
        pltpu.VMEM((4, 8, 8, 16, HD), BF),
        pltpu.VMEM((4, 8, 8, 16, HD), BF),
        pltpu.VMEM((3, 8, 8, 16, HD), BF),
        pltpu.VMEM((8, 8, 16, HD), BF),
        pltpu.VMEM((7, 8, 16, HD), BF),
        pltpu.VMEM((8, 16, HD), BF),
        pltpu.VMEM((7, 16, HD), BF),
        pltpu.VMEM((2, 8, 4, 4, 16, HD), BF),
        pltpu.VMEM((8, 4, 4, 16, HD), BF),
        pltpu.VMEM((8, 4, 4, 16, HD), BF),
        pltpu.VMEM((7, 4, 4, 16, HD), BF),
        pltpu.VMEM((4, 4, 16, HD), BF),
        pltpu.VMEM((3, 4, 16, HD), BF),
        pltpu.VMEM((4, 16, HD), BF),
        pltpu.VMEM((7, 16, HD), BF),
        pltpu.VMEM((16, HD), F32),
        dma((7,)),
    ]
    for n in (halos, 7, 16, 15, 3, 3, 7, 7, 7, 3, 7):
        scratch += [dma((n,)), dma((n,))]
    return pl.pallas_call(
        kernel,
        out_shape=(jax.ShapeDtypeStruct((16, HD), F32), jax.ShapeDtypeStruct((8, HD), F32)),
        in_specs=[any_spec] * 7,
        out_specs=(vmem, vmem),
        scratch_shapes=scratch,
        compiler_params=pltpu.CompilerParams(
            collective_id=0, has_side_effects=True, vmem_limit_bytes=48 * 1024 * 1024
        ),
        name="backward",
    )(hid, q, k, v, g, docs, proj)


def adam_update(first_moment, second_moment, gradient):
    first_new = beta_first * first_moment + (1.0 - beta_first) * gradient
    second_new = beta_second * second_moment + (1.0 - beta_second) * gradient * gradient
    corrected_first = first_new / (1.0 - beta_first**ADAM_STEP)
    corrected_second = second_new / (1.0 - beta_second**ADAM_STEP)
    return (first_new, second_new, corrected_first / (jnp.sqrt(corrected_second) + adam_epsilon))


def on_device(
    hidden_in, queries, keys, values, out_grad, doc_ids, projection, mom1_q, mom2_q, mom1_kv, mom2_kv
):
    grad_q, grad_kv = reduced(
        hidden_in[0], queries[0], keys[0], values[0], out_grad[0], doc_ids, projection
    )
    grad_kv = grad_kv.reshape(2, 4, 4, 32).transpose(0, 2, 1, 3).reshape(2, 16, 32)
    return adam_update(mom1_q, mom2_q, grad_q) + adam_update(mom1_kv, mom2_kv, grad_kv)


def solution(mesh):
    in_specs = (
        P("dp", "seq", None),
        P("dp", "seq", None),
        P("dp", "seq", None),
        P("dp", "seq", None),
        P("dp", "seq", None),
        P("dp", "seq"),
        P("dp", None),
        P("dp", "seq"),
        P("dp", "seq"),
        P(None, "dp", "seq"),
        P(None, "dp", "seq"),
    )
    out_specs = (
        P("dp", "seq"),
        P("dp", "seq"),
        P("dp", "seq"),
        P(None, "dp", "seq"),
        P(None, "dp", "seq"),
        P(None, "dp", "seq"),
    )
    return jax.shard_map(
        on_device, mesh=mesh, in_specs=in_specs, out_specs=out_specs, check_vma=False
    )
```

```python
import jax
import jax.numpy as jnp
from jax import lax
from jax.experimental import pallas as pl
from jax.experimental.pallas import tpu as pltpu
from jax.sharding import PartitionSpec as P

H = 32
KVH = 8
HD = 128
RANK = 256
TOK = 128
DEPTH = 8192
ADAM_STEP = 100

beta_first = 0.9
beta_second = 0.999
adam_epsilon = 1e-08

MESH = pl.DeviceIdType.MESH
SIZES = {"core": 2, "x": 4, "y": 8, "z": 8}
BF = jnp.bfloat16
F32 = jnp.float32
QCOLS = H * HD
KCOLS = KVH * HD
PIECES = 4
PIECE = KCOLS // PIECES
BLOCK = 512
HALF = 256
QUARTER = 128


def rem(a, n):
    return lax.rem(a, n)


def here():
    s = lax.axis_index("seq")
    d = lax.axis_index("dp")
    return {
        "core": rem(s, 2),
        "x": rem(s // 2, 4),
        "y": (s // 8) * 2 + rem(d, 2),
        "z": d // 2,
    }


def device(c):
    return {
        "seq": (c["y"] // 2) * 8 + c["x"] * 2 + c["core"],
        "dp": c["z"] * 2 + rem(c["y"], 2),
    }


def moved(c, axis, k):
    n = SIZES[axis]
    out = dict(c)
    out[axis] = rem(c[axis] + (k % n), n)
    return out


def dot_rows(a, b):
    return lax.dot_general(a, b, (((1,), (1,)), ((), ())), preferred_element_type=F32)


def dot_plain(a, b):
    return lax.dot_general(a, b, (((1,), (0,)), ((), ())), preferred_element_type=F32)


def dot_first(a, b):
    return lax.dot_general(a, b, (((0,), (0,)), ((), ())), preferred_element_type=F32)


def kernel(
    hid_in, q_in, k_in, v_in, g_in, doc_in, proj_in,
    outq_ref, outkv_ref,
    hid, q, g, kw, vw, docs, bias, pg, dq, dkv, acc, lr, left, dup, perm,
    zq, rq, xq, xr, yq, yr, wq, wr,
    zk, rk, ck, cr, xk, xkr, yk, ykr, kv_sum,
    relay,
    load_sem,
    rel_send, rel_recv,
    halo_send, halo_recv,
    gz_send, gz_recv, gy_send, gy_recv, gc_send, gc_recv,
    rc_send, rc_recv, qx_send, qx_recv, qy_send, qy_recv, qz_send, qz_recv,
    kz_send, kz_recv, kx_send, kx_recv, ky_send, ky_recv,
):
    c = here()
    s = lax.axis_index("seq")
    d = lax.axis_index("dp")
    core, x, y, z = c["core"], c["x"], c["y"], c["z"]
    y_lo = rem(y, 2)
    nxt = {"seq": rem(s + 1, 32), "dp": d}
    prv = {"seq": rem(s + 31, 32), "dp": d}
    sibling = device(moved(c, "core", 1))
    across = device(
        {"core": 1 - core, "x": rem(x + jnp.where(core == 1, 1, 3), 4), "y": y, "z": z}
    )
    turn = (x == 3) & (core == 1)
    over, back = device(moved(c, "y", 2)), device(moved(c, "y", -2))

    def zstep(k):
        return rem(z + jnp.where(core == 0, k + 8, 8 - k), 8)

    def zdev(k):
        n = dict(c)
        n["z"] = zstep(k)
        return device(n)

    barrier = pltpu.get_barrier_semaphore()
    peers = [nxt, prv, sibling, across]
    for axis in ("x", "y", "z"):
        for k in range(1, SIZES[axis]):
            peers.append(device(moved(c, axis, k)))
    for p in peers:
        pl.semaphore_signal(barrier, inc=1, device_id=p, device_id_type=MESH)

    loads = [
        pltpu.make_async_copy(doc_in, docs.at[0], load_sem.at[0]),
        pltpu.make_async_copy(k_in, kw.at[pl.ds(TOK, TOK)], load_sem.at[1]),
        pltpu.make_async_copy(v_in, vw.at[pl.ds(TOK, TOK)], load_sem.at[2]),
        pltpu.make_async_copy(q_in, q, load_sem.at[3]),
        pltpu.make_async_copy(g_in, g, load_sem.at[4]),
        pltpu.make_async_copy(
            proj_in, pg.at[pl.ds(pl.multiple_of(d * BLOCK, BLOCK), BLOCK)], load_sem.at[5]
        ),
        pltpu.make_async_copy(hid_in, hid, load_sem.at[6]),
    ]
    for cp in loads:
        cp.start()

    pl.semaphore_wait(barrier, len(peers))

    def remote(src, dst, send, recv, to):
        return pltpu.make_async_remote_copy(
            src_ref=src, dst_ref=dst, send_sem=send, recv_sem=recv, device_id=to, device_id_type=MESH
        )

    sent = []

    def go(cp):
        cp.start()
        sent.append(cp)
        return cp

    def prow(w, b, h, u=None):
        if u is None:
            return pg.at[pl.ds(pl.multiple_of((w * 2 + b) * BLOCK + h * HALF, HALF), HALF)]
        return pg.at[pl.ds(pl.multiple_of((w * 2 + b) * BLOCK + h * HALF + u * QUARTER, QUARTER), QUARTER)]

    def own_quarter(u):
        return proj_in.at[pl.ds(pl.multiple_of(core * HALF + u * QUARTER, QUARTER), QUARTER)]

    zf, zb = zdev(1), zdev(-1)
    yu, yd = device(moved(c, "y", 1)), device(moved(c, "y", -1))
    for u in range(2):
        go(remote(own_quarter(u), prow(z, y_lo, core, u), gz_send.at[u], gz_recv.at[u], zf))
        go(remote(own_quarter(u), prow(z, y_lo, core, u), gz_send.at[8 + u], gz_recv.at[8 + u], zb))
    def halo_copy(t, i, to, src=None):
        cols = pl.ds(i * PIECE, PIECE)
        slot = t * PIECES + i
        at = (kw, vw)[t].at[pl.ds(0, TOK), cols]
        return remote((k_in, v_in)[t].at[:, cols] if src is None else src, at, halo_send.at[slot], halo_recv.at[slot], to)

    def relay_copy(t, i):
        cols = pl.ds(i * PIECE, PIECE)
        slot = t * 2 + i - 2
        return remote((k_in, v_in)[t].at[:, cols], relay.at[slot], rel_send.at[slot], rel_recv.at[slot], over)

    def pass_on(t, i):
        return halo_copy(t, i, across, relay.at[t * 2 + i - 2])

    loads[0].wait()
    docs_copy = go(remote(docs.at[0], docs.at[1], halo_send.at[2 * PIECES], halo_recv.at[2 * PIECES], nxt))
    for i in range(2):
        for t in range(2):
            go(halo_copy(t, i, nxt))

    @pl.when(turn)
    def _():
        for i in (2, 3):
            for t in range(2):
                relay_copy(t, i).start()

    @pl.when(jnp.logical_not(turn))
    def _():
        for i in (2, 3):
            for t in range(2):
                halo_copy(t, i, nxt).start()

    def relay_pass(i):
        @pl.when(turn)
        def _():
            for t in range(2):
                relay_copy(t, i).wait_recv()
                pass_on(t, i).start()

    def halo_wait(i):
        for t in range(2):
            halo_copy(t, i, nxt).wait_recv()

    def halo_sent():
        @pl.when(turn)
        def _():
            for i in (2, 3):
                for t in range(2):
                    relay_copy(t, i).wait_send()
                    pass_on(t, i).wait_send()

        @pl.when(jnp.logical_not(turn))
        def _():
            for i in (2, 3):
                for t in range(2):
                    halo_copy(t, i, nxt).wait_send()

    ahead = [0, 1, -1, 2, -2, 3, -3, 4]

    def y_way(j, u):
        return j not in (0, 2) and (j % 2 == 1) == (u == 0)

    def y_send(j, u, src):
        ref = prow(zstep(-ahead[j]), y_lo, core, u)
        go(remote(src, ref, gy_send.at[2 * j + u], gy_recv.at[2 * j + u], yu if y_way(j, u) else yd))

    for u in range(2):
        y_send(0, u, own_quarter(u))

    def core_send(slot, w, b):
        ref = prow(w, b, core)
        go(remote(ref, ref, gc_send.at[slot], gc_recv.at[slot], sibling))

    def z_arrival(j, u):
        w = zstep(-ahead[j])
        ref = prow(w, y_lo, core, u)
        k = (j - 1) // 2
        slot = 2 * k + u if j % 2 else 8 + 2 * k + u
        remote(ref, ref, gz_send.at[slot], gz_recv.at[slot], zf).wait_recv()
        if j < 6:
            go(remote(ref, ref, gz_send.at[slot + 2], gz_recv.at[slot + 2], zf if j % 2 else zb))
        y_send(j, u, ref)
        if u:
            core_send(j - 1, w, y_lo)

    def y_arrival(j):
        w = zstep(-ahead[j])
        for u in range(2):
            ref = prow(w, 1 - y_lo, core, u)
            remote(ref, ref, gy_send.at[2 * j + u], gy_recv.at[2 * j + u], yu).wait_recv()
        core_send(7 + j, w, 1 - y_lo)

    def core_arrival(slot):
        w, b = (zstep(ahead[slot + 1]), y_lo) if slot < 7 else (zstep(ahead[slot - 7]), 1 - y_lo)
        ref = prow(w, b, 1 - core)
        remote(ref, ref, gc_send.at[slot], gc_recv.at[slot], sibling).wait_recv()

    def low_part(w, b, h):
        at = pl.multiple_of((w * 2 + b) * BLOCK + h * HALF, HALF)
        return dot_plain(hid[:, pl.ds(at, HALF)], pg[pl.ds(at, HALF)])

    def low_core(slot):
        w, b = (zstep(ahead[slot + 1]), y_lo) if slot < 7 else (zstep(ahead[slot - 7]), 1 - y_lo)
        return low_part(w, b, 1 - core)

    def add_low(parts):
        tot = parts[0]
        for p in parts[1:]:
            tot = tot + p
        acc[...] += tot

    score_scale = 1.0 / HD**0.5

    def attend(gi):
        wide = pl.multiple_of(gi * 512, 512)
        thin = pl.multiple_of(gi * HD, HD)
        qh = [q[:, pl.ds(wide + j * HD, HD)] for j in range(4)]
        gh = [g[:, pl.ds(wide + j * HD, HD)] for j in range(4)]
        q4 = jnp.concatenate(qh, axis=0)
        g4 = jnp.concatenate(gh, axis=0)
        kwin = kw[:, pl.ds(thin, HD)]
        vwin = vw[:, pl.ds(thin, HD)]
        sc = dot_rows(q4, kwin).reshape(4, TOK, 256) * score_scale + bias[...][None]
        sc = sc.reshape(512, 256)
        peak = jnp.max(sc, axis=1, keepdims=True)
        e = jnp.exp(sc - peak)
        att = e * (1.0 / jnp.sum(e, axis=1, keepdims=True))
        low = att.astype(BF)
        da = dot_rows(g4, vwin)
        delta = jnp.sum(low.astype(F32) * da, axis=1, keepdims=True)
        ds = (att * (da - delta)).astype(BF)
        dqv = (dot_plain(ds, kwin) * score_scale).astype(BF)
        for j in range(4):
            dq[:, pl.ds(wide + j * HD, HD)] = dqv[j * TOK : (j + 1) * TOK]
        dkv[pl.ds(0, 2 * TOK), pl.ds(thin, HD)] = (dot_first(ds, q4) * score_scale).astype(BF)
        dkv[pl.ds(2 * TOK, 2 * TOK), pl.ds(thin, HD)] = dot_first(low, g4).astype(BF)

    docs_copy.wait_recv()
    mine = jnp.broadcast_to(docs[0].astype(F32), (TOK, TOK))
    before = jnp.broadcast_to(docs[1].astype(F32), (TOK, TOK))
    before = jnp.where(s == 0, -1.0, before)
    rows = jnp.transpose(mine)
    causal = lax.broadcasted_iota(jnp.int32, (TOK, TOK), 1) <= lax.broadcasted_iota(jnp.int32, (TOK, TOK), 0)
    bias[:, TOK:] = jnp.where(causal & (mine == rows), 0.0, -jnp.inf)
    bias[:, :TOK] = jnp.where(before == rows, 0.0, -jnp.inf)

    for cp in loads[1:5]:
        cp.wait()
    z_arrival(1, 0)
    z_arrival(2, 0)
    halo_wait(0)
    attend(0)
    z_arrival(1, 1)
    z_arrival(2, 1)
    y_arrival(0)
    attend(1)
    relay_pass(2)
    z_arrival(3, 0)
    z_arrival(4, 0)
    halo_wait(1)
    attend(2)
    relay_pass(3)
    z_arrival(3, 1)
    z_arrival(4, 1)
    y_arrival(1)
    attend(3)
    z_arrival(5, 0)
    z_arrival(6, 0)
    y_arrival(2)
    halo_wait(2)
    attend(4)
    z_arrival(5, 1)
    z_arrival(6, 1)
    attend(5)
    z_arrival(7, 0)
    y_arrival(3)
    halo_wait(3)
    attend(6)
    z_arrival(7, 1)
    y_arrival(4)
    attend(7)
    y_arrival(5)
    ri = lax.broadcasted_iota(jnp.int32, (512, RANK), 0)
    ci = lax.broadcasted_iota(jnp.int32, (512, RANK), 1)
    want = ((ri & 127) >> 3) * 16 + (ri >> 7) * 4 + (ri & 3)
    dup[...] = jnp.where(ci == want, 1.0, 0.0).astype(BF)
    ri = lax.broadcasted_iota(jnp.int32, (512, 512), 0)
    ci = lax.broadcasted_iota(jnp.int32, (512, 512), 1)
    want = ((ci & 127) >> 5) * 128 + (ci >> 7) * 32 + (ci & 31)
    perm[...] = jnp.where(ri == want, 1.0, 0.0).astype(BF)

    loads[5].wait()
    loads[6].wait()
    at = pl.multiple_of(d * BLOCK, BLOCK)
    acc[...] = dot_plain(hid[:, pl.ds(at, BLOCK)], pg[pl.ds(at, BLOCK)])
    add_low([low_part(zstep(-ahead[j]), y_lo, core) for j in range(1, 8)])
    y_arrival(6)
    add_low([low_part(zstep(-ahead[j]), 1 - y_lo, core) for j in range(7)])
    y_arrival(7)
    order = [0, 1, 7, 2, 3, 8, 9, 4, 10, 11, 5, 6, 12, 13, 14]
    add_low([low_part(zstep(-ahead[7]), 1 - y_lo, core)])
    for some in (order[:9], order[9:13], order[13:]):
        for slot in some:
            core_arrival(slot)
        add_low([low_core(slot) for slot in some])

    lr[pl.ds(TOK, TOK)] = acc[...].astype(BF)
    lr_copy = go(
        remote(lr.at[pl.ds(TOK, TOK)], lr.at[pl.ds(0, TOK)], halo_send.at[2 * PIECES + 1], halo_recv.at[2 * PIECES + 1], nxt)
    )
    turned = jnp.transpose(acc[...]).astype(BF)

    def project(gi):
        part = dot_plain(turned, dq[:, pl.ds(pl.multiple_of(gi * 512, 512), 512)]).astype(BF)
        for j in range(4):
            piece = part[:, j * HD : (j + 1) * HD].reshape(8, 2, 16, HD)
            at_x = rem(2 * gi + j // 2, 4)
            for lo in range(2):
                zq[j % 2, at_x, (gi // 2) * 2 + lo] = piece[:, lo]

    def project_even(i, carry):
        project(2 * i)
        return carry

    def project_odd(i, carry):
        project(2 * i + 1)
        return carry

    lax.fori_loop(0, 4, project_even, 0)
    qc = [go(remote(zq.at[1 - core, pl.ds(0, 2)], rq.at[pl.ds(0, 2)], rc_send.at[0], rc_recv.at[0], sibling))]
    lax.fori_loop(0, 4, project_odd, 0)
    qc.append(go(remote(zq.at[1 - core, pl.ds(2, 2)], rq.at[pl.ds(2, 2)], rc_send.at[1], rc_recv.at[1], sibling)))

    for cp in qc:
        cp.wait_recv()
    qx = []
    for k in (2, 1, 3, 0):
        at = rem(x + k, 4)
        xq[at] = (zq[core, at].astype(F32) + rq[at].astype(F32)).astype(BF)
        if k:
            qx.append(go(remote(xq.at[at], xr.at[k - 1], qx_send.at[k - 1], qx_recv.at[k - 1], device(moved(c, "x", k)))))

    lr_copy.wait_recv()
    spread = dot_rows(dup[...], lr[...])
    kind = (lax.broadcasted_iota(jnp.int32, (512, 256), 0) >> 2) & 1
    left[:, : 2 * TOK] = jnp.where(kind == 0, spread, 0.0).astype(BF)
    left[:, 2 * TOK :] = jnp.where(kind == 1, spread, 0.0).astype(BF)
    for a in range(0, KVH, 2):
        both = dot_plain(left[...], dkv[:, a * HD : (a + 2) * HD]).astype(BF)
        for t in range(2):
            wide = jnp.concatenate(
                [both[i * 128 : (i + 1) * 128, t * HD : (t + 1) * HD] for i in range(4)], axis=1
            )
            wide = dot_plain(wide, perm[...]).astype(BF)
            for b in range(4):
                zk[b % 2, :, t * 2 + b // 2, a // 2] = wide[:, b * HD : (b + 1) * HD].reshape(8, 16, HD)
    kc = go(remote(zk.at[1 - core], rk, rc_send.at[2], rc_recv.at[2], sibling))

    kc.wait_recv()
    kz = []
    for k in (4, 3, 5, 2, 6, 1, 7, 0):
        at = rem(z + k, 8)
        ck[at] = (zk[core, at].astype(F32) + rk[at].astype(F32)).astype(BF)
        if k:
            kz.append(go(remote(ck.at[at], cr.at[k - 1], kz_send.at[k - 1], kz_recv.at[k - 1], device(moved(c, "z", k)))))

    for cp in qx:
        cp.wait_recv()
    qy = []
    for k in (4, 3, 5, 2, 6, 1, 7, 0):
        at = rem(y + k, 8)
        tot = xq[x, at].astype(F32)
        for i in range(3):
            tot = tot + xr[i, at].astype(F32)
        yq[at] = tot.astype(BF)
        if k:
            qy.append(go(remote(yq.at[at], yr.at[k - 1], qy_send.at[k - 1], qy_recv.at[k - 1], device(moved(c, "y", k)))))
    for cp in kz:
        cp.wait_recv()
    kx = []
    for k in (2, 1, 3, 0):
        at = rem(x + k, 4)
        tot = ck[z, at].astype(F32)
        for i in range(7):
            tot = tot + cr[i, at].astype(F32)
        xk[at] = tot.astype(BF)
        if k:
            kx.append(go(remote(xk.at[at], xkr.at[k - 1], kx_send.at[k - 1], kx_recv.at[k - 1], device(moved(c, "x", k)))))
    for cp in qy:
        cp.wait_recv()
    tot = yq[y].astype(F32)
    for i in range(7):
        tot = tot + yr[i].astype(F32)
    wq[...] = tot.astype(BF)
    qz = []
    for k in (4, 3, 5, 2, 6, 1, 7):
        at = rem(z + k, 8)
        qz.append(go(remote(wq.at[at], wr.at[k - 1], qz_send.at[k - 1], qz_recv.at[k - 1], device(moved(c, "z", k)))))
    for cp in kx:
        cp.wait_recv()
    tot = xk[x].astype(F32)
    for i in range(3):
        tot = tot + xkr[i].astype(F32)
    yk[...] = tot.astype(BF)
    ky = []
    for k in (4, 3, 5, 2, 6, 1, 7):
        to = moved(c, "y", k)
        ky.append(go(remote(yk.at[to["y"] // 2], ykr.at[k - 1], ky_send.at[k - 1], ky_recv.at[k - 1], device(to))))
    for cp in qz:
        cp.wait_recv()
    tot = wq[z].astype(F32)
    for i in range(7):
        tot = tot + wr[i].astype(F32)
    outq_ref[...] = tot
    for cp in ky:
        cp.wait_recv()
    tot = yk[y // 2].astype(F32)
    for i in range(7):
        tot = tot + ykr[i].astype(F32)
    kv_sum[...] = tot
    outkv_ref[...] = kv_sum[pl.ds(pl.multiple_of(y_lo * 8, 8), 8)]
    for cp in sent:
        cp.wait_send()
    halo_sent()


def reduced(hid, q, k, v, g, docs, proj):
    any_spec = pl.BlockSpec(memory_space=pltpu.HBM)
    vmem = pl.BlockSpec(memory_space=pltpu.VMEM)
    dma = pltpu.SemaphoreType.DMA
    halos = 2 * PIECES + 2
    scratch = [
        pltpu.VMEM((TOK, DEPTH), BF),
        pltpu.VMEM((TOK, QCOLS), BF),
        pltpu.VMEM((TOK, QCOLS), BF),
        pltpu.VMEM((2 * TOK, KCOLS), BF),
        pltpu.VMEM((2 * TOK, KCOLS), BF),
        pltpu.VMEM((2, 1, TOK), jnp.int32),
        pltpu.VMEM((TOK, 2 * TOK), F32),
        pltpu.VMEM((DEPTH, RANK), BF),
        pltpu.VMEM((TOK, QCOLS), BF),
        pltpu.VMEM((4 * TOK, KCOLS), BF),
        pltpu.VMEM((TOK, RANK), F32),
        pltpu.VMEM((2 * TOK, RANK), BF),
        pltpu.VMEM((512, 4 * TOK), BF),
        pltpu.VMEM((512, RANK), BF),
        pltpu.VMEM((512, 512), BF),
        pltpu.VMEM((2, 4, 8, 8, 16, HD), BF),
        pltpu.VMEM((4, 8, 8, 16, HD), BF),
        pltpu.VMEM((4, 8, 8, 16, HD), BF),
        pltpu.VMEM((3, 8, 8, 16, HD), BF),
        pltpu.VMEM((8, 8, 16, HD), BF),
        pltpu.VMEM((7, 8, 16, HD), BF),
        pltpu.VMEM((8, 16, HD), BF),
        pltpu.VMEM((7, 16, HD), BF),
        pltpu.VMEM((2, 8, 4, 4, 16, HD), BF),
        pltpu.VMEM((8, 4, 4, 16, HD), BF),
        pltpu.VMEM((8, 4, 4, 16, HD), BF),
        pltpu.VMEM((7, 4, 4, 16, HD), BF),
        pltpu.VMEM((4, 4, 16, HD), BF),
        pltpu.VMEM((3, 4, 16, HD), BF),
        pltpu.VMEM((4, 16, HD), BF),
        pltpu.VMEM((7, 16, HD), BF),
        pltpu.VMEM((16, HD), F32),
        pltpu.VMEM((4, TOK, PIECE), BF),
        dma((7,)),
    ]
    for n in (4, halos, 14, 16, 15, 3, 3, 7, 7, 7, 3, 7):
        scratch += [dma((n,)), dma((n,))]
    return pl.pallas_call(
        kernel,
        out_shape=(jax.ShapeDtypeStruct((16, HD), F32), jax.ShapeDtypeStruct((8, HD), F32)),
        in_specs=[any_spec] * 7,
        out_specs=(vmem, vmem),
        scratch_shapes=scratch,
        compiler_params=pltpu.CompilerParams(
            collective_id=0, has_side_effects=True, vmem_limit_bytes=62 * 1024 * 1024
        ),
        name="backward",
    )(hid, q, k, v, g, docs, proj)


def adam_update(first_moment, second_moment, gradient):
    first_new = beta_first * first_moment + (1.0 - beta_first) * gradient
    second_new = beta_second * second_moment + (1.0 - beta_second) * gradient * gradient
    corrected_first = first_new / (1.0 - beta_first**ADAM_STEP)
    corrected_second = second_new / (1.0 - beta_second**ADAM_STEP)
    return (first_new, second_new, corrected_first / (jnp.sqrt(corrected_second) + adam_epsilon))


def on_device(
    hidden_in, queries, keys, values, out_grad, doc_ids, projection, mom1_q, mom2_q, mom1_kv, mom2_kv
):
    grad_q, grad_kv = reduced(
        hidden_in[0], queries[0], keys[0], values[0], out_grad[0], doc_ids, projection
    )
    grad_kv = grad_kv.reshape(2, 4, 4, 32).transpose(0, 2, 1, 3).reshape(2, 16, 32)
    return adam_update(mom1_q, mom2_q, grad_q) + adam_update(mom1_kv, mom2_kv, grad_kv)


def solution(mesh):
    in_specs = (
        P("dp", "seq", None),
        P("dp", "seq", None),
        P("dp", "seq", None),
        P("dp", "seq", None),
        P("dp", "seq", None),
        P("dp", "seq"),
        P("dp", None),
        P("dp", "seq"),
        P("dp", "seq"),
        P(None, "dp", "seq"),
        P(None, "dp", "seq"),
    )
    out_specs = (
        P("dp", "seq"),
        P("dp", "seq"),
        P("dp", "seq"),
        P(None, "dp", "seq"),
        P(None, "dp", "seq"),
        P(None, "dp", "seq"),
    )
    return jax.shard_map(
        on_device, mesh=mesh, in_specs=in_specs, out_specs=out_specs, check_vma=False
    )
```

```python
import jax
import jax.numpy as jnp
from jax import lax
from jax.experimental import pallas as pl
from jax.experimental.pallas import tpu as pltpu
from jax.sharding import PartitionSpec as P

H = 32
KVH = 8
HD = 128
RANK = 256
TOK = 128
DEPTH = 8192
ADAM_STEP = 100

beta_first = 0.9
beta_second = 0.999
adam_epsilon = 1e-08

MESH = pl.DeviceIdType.MESH
SIZES = {"core": 2, "x": 4, "y": 8, "z": 8}
BF = jnp.bfloat16
F32 = jnp.float32
QCOLS = H * HD
KCOLS = KVH * HD
PIECES = 4
PIECE = KCOLS // PIECES
BLOCK = 512
HALF = 256
QUARTER = 128
FAR = 6


def rem(a, n):
    return lax.rem(a, n)


def here():
    s = lax.axis_index("seq")
    d = lax.axis_index("dp")
    return {
        "core": rem(s, 2),
        "x": rem(s // 2, 4),
        "y": (s // 8) * 2 + rem(d, 2),
        "z": d // 2,
    }


def device(c):
    return {
        "seq": (c["y"] // 2) * 8 + c["x"] * 2 + c["core"],
        "dp": c["z"] * 2 + rem(c["y"], 2),
    }


def moved(c, axis, k):
    n = SIZES[axis]
    out = dict(c)
    out[axis] = rem(c[axis] + (k % n), n)
    return out


def dot_rows(a, b):
    return lax.dot_general(a, b, (((1,), (1,)), ((), ())), preferred_element_type=F32)


def dot_plain(a, b):
    return lax.dot_general(a, b, (((1,), (0,)), ((), ())), preferred_element_type=F32)


def dot_first(a, b):
    return lax.dot_general(a, b, (((0,), (0,)), ((), ())), preferred_element_type=F32)


def kernel(
    hid_in, q_in, k_in, v_in, g_in, doc_in, proj_in,
    outq_ref, outkv_ref,
    hid, q, g, kw, vw, docs, bias, pg, dq, dkv, acc, lr, left, dup, perm,
    zq, rq, xq, xr, yq, yr, wq, wr,
    zk, rk, ck, cr, xk, xkr, yk, ykr, kv_sum,
    relay, cb, cbr, db, dbr, qb, qbr, qc2, qcr,
    load_sem,
    by_send, by_recv, bqx_send, bqx_recv,
    bx_send, bx_recv, bz_send, bz_recv,
    rel_send, rel_recv,
    halo_send, halo_recv,
    gz_send, gz_recv, gy_send, gy_recv, gc_send, gc_recv,
    rc_send, rc_recv, qx_send, qx_recv, qy_send, qy_recv, qz_send, qz_recv,
    kz_send, kz_recv, kx_send, kx_recv, ky_send, ky_recv,
):
    c = here()
    s = lax.axis_index("seq")
    d = lax.axis_index("dp")
    core, x, y, z = c["core"], c["x"], c["y"], c["z"]
    y_lo = rem(y, 2)
    nxt = {"seq": rem(s + 1, 32), "dp": d}
    prv = {"seq": rem(s + 31, 32), "dp": d}
    sibling = device(moved(c, "core", 1))
    across = device(
        {"core": 1 - core, "x": rem(x + jnp.where(core == 1, 1, 3), 4), "y": y, "z": z}
    )
    turn = (x == 3) & (core == 1)
    over, back = device(moved(c, "y", 2)), device(moved(c, "y", -2))

    def zstep(k):
        return rem(z + jnp.where(core == 0, k + 8, 8 - k), 8)

    def zdev(k):
        n = dict(c)
        n["z"] = zstep(k)
        return device(n)

    barrier = pltpu.get_barrier_semaphore()
    peers = [nxt, prv, sibling, across]
    for axis in ("x", "y", "z"):
        for k in range(1, SIZES[axis]):
            peers.append(device(moved(c, axis, k)))
    for p in peers:
        pl.semaphore_signal(barrier, inc=1, device_id=p, device_id_type=MESH)

    loads = [
        pltpu.make_async_copy(doc_in, docs.at[0], load_sem.at[0]),
        pltpu.make_async_copy(k_in, kw.at[pl.ds(TOK, TOK)], load_sem.at[1]),
        pltpu.make_async_copy(v_in, vw.at[pl.ds(TOK, TOK)], load_sem.at[2]),
        pltpu.make_async_copy(q_in, q, load_sem.at[3]),
        pltpu.make_async_copy(g_in, g, load_sem.at[4]),
        pltpu.make_async_copy(
            proj_in, pg.at[pl.ds(pl.multiple_of(d * BLOCK, BLOCK), BLOCK)], load_sem.at[5]
        ),
        pltpu.make_async_copy(hid_in, hid, load_sem.at[6]),
    ]
    for cp in loads:
        cp.start()

    pl.semaphore_wait(barrier, len(peers))

    def remote(src, dst, send, recv, to):
        return pltpu.make_async_remote_copy(
            src_ref=src, dst_ref=dst, send_sem=send, recv_sem=recv, device_id=to, device_id_type=MESH
        )

    sent = []

    def go(cp):
        cp.start()
        sent.append(cp)
        return cp

    def prow(w, b, h, u=None):
        if u is None:
            return pg.at[pl.ds(pl.multiple_of((w * 2 + b) * BLOCK + h * HALF, HALF), HALF)]
        return pg.at[pl.ds(pl.multiple_of((w * 2 + b) * BLOCK + h * HALF + u * QUARTER, QUARTER), QUARTER)]

    def own_quarter(u):
        return proj_in.at[pl.ds(pl.multiple_of(core * HALF + u * QUARTER, QUARTER), QUARTER)]

    zf, zb = zdev(1), zdev(-1)
    yu, yd = device(moved(c, "y", 1)), device(moved(c, "y", -1))
    for u in range(2):
        go(remote(own_quarter(u), prow(z, y_lo, core, u), gz_send.at[u], gz_recv.at[u], zf))
        go(remote(own_quarter(u), prow(z, y_lo, core, u), gz_send.at[8 + u], gz_recv.at[8 + u], zb))
    def halo_copy(t, i, to, src=None):
        cols = pl.ds(i * PIECE, PIECE)
        slot = t * PIECES + i
        at = (kw, vw)[t].at[pl.ds(0, TOK), cols]
        return remote((k_in, v_in)[t].at[:, cols] if src is None else src, at, halo_send.at[slot], halo_recv.at[slot], to)

    def relay_copy(t, i):
        cols = pl.ds(i * PIECE, PIECE)
        slot = t * 2 + i - 2
        return remote((k_in, v_in)[t].at[:, cols], relay.at[slot], rel_send.at[slot], rel_recv.at[slot], over)

    def pass_on(t, i):
        return halo_copy(t, i, across, relay.at[t * 2 + i - 2])

    loads[0].wait()
    docs_copy = go(remote(docs.at[0], docs.at[1], halo_send.at[2 * PIECES], halo_recv.at[2 * PIECES], nxt))
    for i in range(2):
        for t in range(2):
            go(halo_copy(t, i, nxt))

    @pl.when(turn)
    def _():
        for i in (2, 3):
            for t in range(2):
                relay_copy(t, i).start()

    @pl.when(jnp.logical_not(turn))
    def _():
        for i in (2, 3):
            for t in range(2):
                halo_copy(t, i, nxt).start()

    def relay_pass(i):
        @pl.when(turn)
        def _():
            for t in range(2):
                relay_copy(t, i).wait_recv()
                pass_on(t, i).start()

    def halo_wait(i):
        for t in range(2):
            halo_copy(t, i, nxt).wait_recv()

    def halo_sent():
        @pl.when(turn)
        def _():
            for i in (2, 3):
                for t in range(2):
                    relay_copy(t, i).wait_send()
                    pass_on(t, i).wait_send()

        @pl.when(jnp.logical_not(turn))
        def _():
            for i in (2, 3):
                for t in range(2):
                    halo_copy(t, i, nxt).wait_send()

    ahead = [0, 1, -1, 2, -2, 3, -3, 4]

    def y_way(j, u):
        return j not in (0, 2) and (j % 2 == 1) == (u == 0)

    def y_send(j, u, src):
        ref = prow(zstep(-ahead[j]), y_lo, core, u)
        go(remote(src, ref, gy_send.at[2 * j + u], gy_recv.at[2 * j + u], yu if y_way(j, u) else yd))

    for u in range(2):
        y_send(0, u, own_quarter(u))

    def core_send(slot, w, b):
        ref = prow(w, b, core)
        go(remote(ref, ref, gc_send.at[slot], gc_recv.at[slot], sibling))

    def z_arrival(j, u):
        w = zstep(-ahead[j])
        ref = prow(w, y_lo, core, u)
        k = (j - 1) // 2
        slot = 2 * k + u if j % 2 else 8 + 2 * k + u
        remote(ref, ref, gz_send.at[slot], gz_recv.at[slot], zf).wait_recv()
        if j < 6:
            go(remote(ref, ref, gz_send.at[slot + 2], gz_recv.at[slot + 2], zf if j % 2 else zb))
        y_send(j, u, ref)
        if u:
            core_send(j - 1, w, y_lo)

    def y_arrival(j):
        w = zstep(-ahead[j])
        for u in range(2):
            ref = prow(w, 1 - y_lo, core, u)
            remote(ref, ref, gy_send.at[2 * j + u], gy_recv.at[2 * j + u], yu).wait_recv()
        core_send(7 + j, w, 1 - y_lo)

    def core_arrival(slot):
        w, b = (zstep(ahead[slot + 1]), y_lo) if slot < 7 else (zstep(ahead[slot - 7]), 1 - y_lo)
        ref = prow(w, b, 1 - core)
        remote(ref, ref, gc_send.at[slot], gc_recv.at[slot], sibling).wait_recv()

    def low_part(w, b, h):
        at = pl.multiple_of((w * 2 + b) * BLOCK + h * HALF, HALF)
        return dot_plain(hid[:, pl.ds(at, HALF)], pg[pl.ds(at, HALF)])

    def low_core(slot):
        w, b = (zstep(ahead[slot + 1]), y_lo) if slot < 7 else (zstep(ahead[slot - 7]), 1 - y_lo)
        return low_part(w, b, 1 - core)

    def add_low(parts):
        tot = parts[0]
        for p in parts[1:]:
            tot = tot + p
        acc[...] += tot

    score_scale = 1.0 / HD**0.5

    def attend(gi):
        wide = pl.multiple_of(gi * 512, 512)
        thin = pl.multiple_of(gi * HD, HD)
        qh = [q[:, pl.ds(wide + j * HD, HD)] for j in range(4)]
        gh = [g[:, pl.ds(wide + j * HD, HD)] for j in range(4)]
        q4 = jnp.concatenate(qh, axis=0)
        g4 = jnp.concatenate(gh, axis=0)
        kwin = kw[:, pl.ds(thin, HD)]
        vwin = vw[:, pl.ds(thin, HD)]
        sc = dot_rows(q4, kwin).reshape(4, TOK, 256) * score_scale + bias[...][None]
        sc = sc.reshape(512, 256)
        peak = jnp.max(sc, axis=1, keepdims=True)
        e = jnp.exp(sc - peak)
        att = e * (1.0 / jnp.sum(e, axis=1, keepdims=True))
        low = att.astype(BF)
        da = dot_rows(g4, vwin)
        delta = jnp.sum(low.astype(F32) * da, axis=1, keepdims=True)
        ds = (att * (da - delta)).astype(BF)
        dqv = (dot_plain(ds, kwin) * score_scale).astype(BF)
        for j in range(4):
            dq[:, pl.ds(wide + j * HD, HD)] = dqv[j * TOK : (j + 1) * TOK]
        dkv[pl.ds(0, 2 * TOK), pl.ds(thin, HD)] = (dot_first(ds, q4) * score_scale).astype(BF)
        dkv[pl.ds(2 * TOK, 2 * TOK), pl.ds(thin, HD)] = dot_first(low, g4).astype(BF)

    ri = lax.broadcasted_iota(jnp.int32, (512, RANK), 0)
    ci = lax.broadcasted_iota(jnp.int32, (512, RANK), 1)
    want = ((ri & 127) >> 3) * 16 + (ri >> 7) * 4 + (ri & 3)
    dup[...] = jnp.where(ci == want, 1.0, 0.0).astype(BF)
    ri = lax.broadcasted_iota(jnp.int32, (512, 512), 0)
    ci = lax.broadcasted_iota(jnp.int32, (512, 512), 1)
    want = ((ci & 127) >> 5) * 128 + (ci >> 7) * 32 + (ci & 31)
    perm[...] = jnp.where(ri == want, 1.0, 0.0).astype(BF)

    docs_copy.wait_recv()
    mine = jnp.broadcast_to(docs[0].astype(F32), (TOK, TOK))
    before = jnp.broadcast_to(docs[1].astype(F32), (TOK, TOK))
    before = jnp.where(s == 0, -1.0, before)
    rows = jnp.transpose(mine)
    causal = lax.broadcasted_iota(jnp.int32, (TOK, TOK), 1) <= lax.broadcasted_iota(jnp.int32, (TOK, TOK), 0)
    bias[:, TOK:] = jnp.where(causal & (mine == rows), 0.0, -jnp.inf)
    bias[:, :TOK] = jnp.where(before == rows, 0.0, -jnp.inf)

    for cp in loads[1:5]:
        cp.wait()
    z_arrival(1, 0)
    z_arrival(2, 0)
    halo_wait(0)
    attend(0)
    z_arrival(1, 1)
    z_arrival(2, 1)
    y_arrival(0)
    attend(1)
    relay_pass(2)
    z_arrival(3, 0)
    z_arrival(4, 0)
    halo_wait(1)
    attend(2)
    relay_pass(3)
    z_arrival(3, 1)
    z_arrival(4, 1)
    y_arrival(1)
    attend(3)
    z_arrival(5, 0)
    z_arrival(6, 0)
    y_arrival(2)
    halo_wait(2)
    attend(4)
    z_arrival(5, 1)
    z_arrival(6, 1)
    attend(5)
    z_arrival(7, 0)
    y_arrival(3)
    halo_wait(3)
    attend(6)
    z_arrival(7, 1)
    y_arrival(4)
    attend(7)
    y_arrival(5)
    loads[5].wait()
    loads[6].wait()
    at = pl.multiple_of(d * BLOCK, BLOCK)
    acc[...] = dot_plain(hid[:, pl.ds(at, BLOCK)], pg[pl.ds(at, BLOCK)])
    add_low([low_part(zstep(-ahead[j]), y_lo, core) for j in range(1, 8)])
    y_arrival(6)
    add_low([low_part(zstep(-ahead[j]), 1 - y_lo, core) for j in range(7)])
    y_arrival(7)
    order = [0, 1, 7, 2, 3, 8, 9, 4, 10, 11, 5, 6, 12, 13, 14]
    add_low([low_part(zstep(-ahead[7]), 1 - y_lo, core)])
    for some in (order[:9], order[9:13], order[13:]):
        for slot in some:
            core_arrival(slot)
        add_low([low_core(slot) for slot in some])

    lr[pl.ds(TOK, TOK)] = acc[...].astype(BF)
    lr_copy = go(
        remote(lr.at[pl.ds(TOK, TOK)], lr.at[pl.ds(0, TOK)], halo_send.at[2 * PIECES + 1], halo_recv.at[2 * PIECES + 1], nxt)
    )
    turned = jnp.transpose(acc[...]).astype(BF)

    def project(gi):
        part = dot_plain(turned, dq[:, pl.ds(pl.multiple_of(gi * 512, 512), 512)]).astype(BF)
        for j in range(4):
            piece = part[:, j * HD : (j + 1) * HD].reshape(8, 2, 16, HD)
            at_x = rem(2 * gi + j // 2, 4)
            for lo in range(2):
                zq[j % 2, at_x, (gi // 2) * 2 + lo] = piece[:, lo]

    def project_even(i, carry):
        project(2 * i)
        return carry

    def project_odd(i, carry):
        project(2 * i + 1)
        return carry

    lax.fori_loop(0, 4, project_even, 0)
    qc = [go(remote(zq.at[1 - core, pl.ds(0, 2)], rq.at[pl.ds(0, 2)], rc_send.at[0], rc_recv.at[0], sibling))]
    lax.fori_loop(0, 4, project_odd, 0)
    qc.append(go(remote(zq.at[1 - core, pl.ds(2, 2)], rq.at[pl.ds(2, 2)], rc_send.at[1], rc_recv.at[1], sibling)))

    lr_copy.wait_recv()
    spread = dot_rows(dup[...], lr[...])
    kind = (lax.broadcasted_iota(jnp.int32, (512, 256), 0) >> 2) & 1
    left[:, : 2 * TOK] = jnp.where(kind == 0, spread, 0.0).astype(BF)
    left[:, 2 * TOK :] = jnp.where(kind == 1, spread, 0.0).astype(BF)
    def qx_copy(at):
        slot = rem(at - x + 3, 4)
        to = device({"core": core, "x": at, "y": y, "z": z})
        part = (pl.ds(0, 8), pl.ds(0, FAR))
        return remote(xq.at[(at, *part)], xr.at[(slot, *part)], qx_send.at[slot], qx_recv.at[slot], to)

    def qx_start(at):
        if at % 2 == 0:
            qc[at // 2].wait_recv()
        both_cores = (zq[core, at].astype(F32) + rq[at].astype(F32)).astype(BF)
        xq[at, :, :FAR] = both_cores[:, :FAR]
        qb[:, at] = both_cores[:, FAR:]

        @pl.when(x != at)
        def _():
            qx_copy(at).start()

    def qx_wait(recv):
        for k in range(1, 4):
            cp = qx_copy(rem(x + k, 4))
            if recv:
                cp.wait_recv()
            else:
                cp.wait_send()

    kc = []
    for a in range(0, KVH, 2):
        both = dot_plain(left[...], dkv[:, a * HD : (a + 2) * HD]).astype(BF)
        for t in range(2):
            wide = jnp.concatenate(
                [both[i * 128 : (i + 1) * 128, t * HD : (t + 1) * HD] for i in range(4)], axis=1
            )
            wide = dot_plain(wide, perm[...]).astype(BF)
            for b in range(4):
                zk[b % 2, a // 2, :, t * 2 + b // 2] = wide[:, b * HD : (b + 1) * HD].reshape(8, 16, HD)
        yh = a // 2
        kc.append(go(remote(zk.at[1 - core, yh], rk.at[yh], rc_send.at[2 + yh], rc_recv.at[2 + yh], sibling)))
        if a < 4:
            qx_start(a)
            qx_start(a + 1)

    by = []
    for k in (4, 3, 5, 2, 6, 1, 7):
        at = rem(y + k, 8)
        by.append(go(remote(qb.at[at], qbr.at[k - 1], by_send.at[k - 1], by_recv.at[k - 1], device(moved(c, "y", k)))))
    for yh in range(2):
        kc[yh].wait_recv()
        ck[:, :, yh] = (zk[core, yh].astype(F32) + rk[yh].astype(F32)).astype(BF)
    kz = []
    for k in (4, 3, 5, 2, 6, 1, 7):
        at = rem(z + k, 8)
        kz.append(go(remote(ck.at[at], cr.at[k - 1], kz_send.at[k - 1], kz_recv.at[k - 1], device(moved(c, "z", k)))))
    for yh in range(2):
        kc[2 + yh].wait_recv()
        for at in range(4):
            cb[at, :, yh] = (zk[core, 2 + yh, :, at].astype(F32) + rk[2 + yh, :, at].astype(F32)).astype(BF)
    bx = []
    for k in (2, 1, 3):
        at = rem(x + k, 4)
        bx.append(go(remote(cb.at[at], cbr.at[k - 1], bx_send.at[k - 1], bx_recv.at[k - 1], device(moved(c, "x", k)))))

    qx_wait(True)
    qy = []
    for k in (4, 3, 5, 2, 6, 1, 7, 0):
        at = rem(y + k, 8)
        tot = xq[x, at, :FAR].astype(F32)
        for i in range(3):
            tot = tot + xr[i, at, :FAR].astype(F32)
        yq[at] = tot.astype(BF)
        if k:
            qy.append(go(remote(yq.at[at], yr.at[k - 1], qy_send.at[k - 1], qy_recv.at[k - 1], device(moved(c, "y", k)))))
    for cp in by:
        cp.wait_recv()
    bqx = []
    for k in (2, 1, 3, 0):
        at = rem(x + k, 4)
        tot = qb[y, at].astype(F32)
        for i in range(7):
            tot = tot + qbr[i, at].astype(F32)
        qc2[at] = tot.astype(BF)
        if k:
            bqx.append(go(remote(qc2.at[at], qcr.at[k - 1], bqx_send.at[k - 1], bqx_recv.at[k - 1], device(moved(c, "x", k)))))
    for cp in bx:
        cp.wait_recv()
    bz = []
    tot = cb[x].astype(F32)
    for i in range(3):
        tot = tot + cbr[i].astype(F32)
    db[...] = tot.astype(BF)
    for k in (4, 3, 5, 2, 6, 1, 7):
        at = rem(z + k, 8)
        bz.append(go(remote(db.at[at], dbr.at[k - 1], bz_send.at[k - 1], bz_recv.at[k - 1], device(moved(c, "z", k)))))
    for cp in kz:
        cp.wait_recv()
    kx = []
    for k in (2, 1, 3, 0):
        at = rem(x + k, 4)
        tot = ck[z, at].astype(F32)
        for i in range(7):
            tot = tot + cr[i, at].astype(F32)
        xk[at] = tot.astype(BF)
        if k:
            kx.append(go(remote(xk.at[at], xkr.at[k - 1], kx_send.at[k - 1], kx_recv.at[k - 1], device(moved(c, "x", k)))))
    for cp in qy:
        cp.wait_recv()
    tot = yq[y].astype(F32)
    for i in range(7):
        tot = tot + yr[i].astype(F32)
    wq[pl.ds(0, FAR)] = tot.astype(BF)
    for cp in bqx:
        cp.wait_recv()
    tot = qc2[x].astype(F32)
    for i in range(3):
        tot = tot + qcr[i].astype(F32)
    wq[pl.ds(FAR, 8 - FAR)] = tot.astype(BF)
    qz = []
    for k in (4, 3, 5, 2, 6, 1, 7):
        at = rem(z + k, 8)
        qz.append(go(remote(wq.at[at], wr.at[k - 1], qz_send.at[k - 1], qz_recv.at[k - 1], device(moved(c, "z", k)))))
    for cp in bz:
        cp.wait_recv()
    tot = db[z].astype(F32)
    for i in range(7):
        tot = tot + dbr[i].astype(F32)
    yk[pl.ds(2, 2)] = tot.astype(BF)
    for cp in kx:
        cp.wait_recv()
    tot = xk[x].astype(F32)
    for i in range(3):
        tot = tot + xkr[i].astype(F32)
    yk[pl.ds(0, 2)] = tot.astype(BF)
    ky = []
    for k in (4, 3, 5, 2, 6, 1, 7):
        to = moved(c, "y", k)
        ky.append(go(remote(yk.at[to["y"] // 2], ykr.at[k - 1], ky_send.at[k - 1], ky_recv.at[k - 1], device(to))))
    for cp in qz:
        cp.wait_recv()
    tot = wq[z].astype(F32)
    for i in range(7):
        tot = tot + wr[i].astype(F32)
    outq_ref[...] = tot
    for cp in ky:
        cp.wait_recv()
    tot = yk[y // 2].astype(F32)
    for i in range(7):
        tot = tot + ykr[i].astype(F32)
    kv_sum[...] = tot
    outkv_ref[...] = kv_sum[pl.ds(pl.multiple_of(y_lo * 8, 8), 8)]
    for cp in sent:
        cp.wait_send()
    halo_sent()
    qx_wait(False)


def reduced(hid, q, k, v, g, docs, proj):
    any_spec = pl.BlockSpec(memory_space=pltpu.HBM)
    vmem = pl.BlockSpec(memory_space=pltpu.VMEM)
    dma = pltpu.SemaphoreType.DMA
    halos = 2 * PIECES + 2
    scratch = [
        pltpu.VMEM((TOK, DEPTH), BF),
        pltpu.VMEM((TOK, QCOLS), BF),
        pltpu.VMEM((TOK, QCOLS), BF),
        pltpu.VMEM((2 * TOK, KCOLS), BF),
        pltpu.VMEM((2 * TOK, KCOLS), BF),
        pltpu.VMEM((2, 1, TOK), jnp.int32),
        pltpu.VMEM((TOK, 2 * TOK), F32),
        pltpu.VMEM((DEPTH, RANK), BF),
        pltpu.VMEM((TOK, QCOLS), BF),
        pltpu.VMEM((4 * TOK, KCOLS), BF),
        pltpu.VMEM((TOK, RANK), F32),
        pltpu.VMEM((2 * TOK, RANK), BF),
        pltpu.VMEM((512, 4 * TOK), BF),
        pltpu.VMEM((512, RANK), BF),
        pltpu.VMEM((512, 512), BF),
        pltpu.VMEM((2, 4, 8, 8, 16, HD), BF),
        pltpu.VMEM((4, 8, 8, 16, HD), BF),
        pltpu.VMEM((4, 8, 8, 16, HD), BF),
        pltpu.VMEM((3, 8, 8, 16, HD), BF),
        pltpu.VMEM((8, FAR, 16, HD), BF),
        pltpu.VMEM((7, FAR, 16, HD), BF),
        pltpu.VMEM((8, 16, HD), BF),
        pltpu.VMEM((7, 16, HD), BF),
        pltpu.VMEM((2, 4, 8, 4, 16, HD), BF),
        pltpu.VMEM((4, 8, 4, 16, HD), BF),
        pltpu.VMEM((8, 4, 2, 16, HD), BF),
        pltpu.VMEM((7, 4, 2, 16, HD), BF),
        pltpu.VMEM((4, 2, 16, HD), BF),
        pltpu.VMEM((3, 2, 16, HD), BF),
        pltpu.VMEM((4, 16, HD), BF),
        pltpu.VMEM((7, 16, HD), BF),
        pltpu.VMEM((16, HD), F32),
        pltpu.VMEM((4, TOK, PIECE), BF),
        pltpu.VMEM((4, 8, 2, 16, HD), BF),
        pltpu.VMEM((3, 8, 2, 16, HD), BF),
        pltpu.VMEM((8, 2, 16, HD), BF),
        pltpu.VMEM((7, 2, 16, HD), BF),
        pltpu.VMEM((8, 4, 8 - FAR, 16, HD), BF),
        pltpu.VMEM((7, 4, 8 - FAR, 16, HD), BF),
        pltpu.VMEM((4, 8 - FAR, 16, HD), BF),
        pltpu.VMEM((3, 8 - FAR, 16, HD), BF),
        dma((7,)),
    ]
    for n in (7, 3, 3, 7, 4, halos, 14, 16, 15, 6, 3, 7, 7, 7, 3, 7):
        scratch += [dma((n,)), dma((n,))]
    return pl.pallas_call(
        kernel,
        out_shape=(jax.ShapeDtypeStruct((16, HD), F32), jax.ShapeDtypeStruct((8, HD), F32)),
        in_specs=[any_spec] * 7,
        out_specs=(vmem, vmem),
        scratch_shapes=scratch,
        compiler_params=pltpu.CompilerParams(
            collective_id=0, has_side_effects=True, vmem_limit_bytes=62 * 1024 * 1024
        ),
        name="backward",
    )(hid, q, k, v, g, docs, proj)


def adam_update(first_moment, second_moment, gradient):
    first_new = beta_first * first_moment + (1.0 - beta_first) * gradient
    second_new = beta_second * second_moment + (1.0 - beta_second) * gradient * gradient
    corrected_first = first_new / (1.0 - beta_first**ADAM_STEP)
    corrected_second = second_new / (1.0 - beta_second**ADAM_STEP)
    return (first_new, second_new, corrected_first / (jnp.sqrt(corrected_second) + adam_epsilon))


def on_device(
    hidden_in, queries, keys, values, out_grad, doc_ids, projection, mom1_q, mom2_q, mom1_kv, mom2_kv
):
    grad_q, grad_kv = reduced(
        hidden_in[0], queries[0], keys[0], values[0], out_grad[0], doc_ids, projection
    )
    grad_kv = grad_kv.reshape(2, 4, 4, 32).transpose(0, 2, 1, 3).reshape(2, 16, 32)
    return adam_update(mom1_q, mom2_q, grad_q) + adam_update(mom1_kv, mom2_kv, grad_kv)


def solution(mesh):
    in_specs = (
        P("dp", "seq", None),
        P("dp", "seq", None),
        P("dp", "seq", None),
        P("dp", "seq", None),
        P("dp", "seq", None),
        P("dp", "seq"),
        P("dp", None),
        P("dp", "seq"),
        P("dp", "seq"),
        P(None, "dp", "seq"),
        P(None, "dp", "seq"),
    )
    out_specs = (
        P("dp", "seq"),
        P("dp", "seq"),
        P("dp", "seq"),
        P(None, "dp", "seq"),
        P(None, "dp", "seq"),
        P(None, "dp", "seq"),
    )
    return jax.shard_map(
        on_device, mesh=mesh, in_specs=in_specs, out_specs=out_specs, check_vma=False
    )
```

```python
import jax
import jax.numpy as jnp
from jax import lax
from jax.experimental import pallas as pl
from jax.experimental.pallas import tpu as pltpu
from jax.sharding import PartitionSpec as P

H = 32
KVH = 8
HD = 128
RANK = 256
TOK = 128
DEPTH = 8192
ADAM_STEP = 100

beta_first = 0.9
beta_second = 0.999
adam_epsilon = 1e-08

MESH = pl.DeviceIdType.MESH
SIZES = {"core": 2, "x": 4, "y": 8, "z": 8}
BF = jnp.bfloat16
F32 = jnp.float32
QCOLS = H * HD
KCOLS = KVH * HD
PIECES = 4
PIECE = KCOLS // PIECES
BLOCK = 512
HALF = 256
QUARTER = 128
FAR = 5


def rem(a, n):
    return lax.rem(a, n)


def here():
    s = lax.axis_index("seq")
    d = lax.axis_index("dp")
    return {
        "core": rem(s, 2),
        "x": rem(s // 2, 4),
        "y": (s // 8) * 2 + rem(d, 2),
        "z": d // 2,
    }


def device(c):
    return {
        "seq": (c["y"] // 2) * 8 + c["x"] * 2 + c["core"],
        "dp": c["z"] * 2 + rem(c["y"], 2),
    }


def moved(c, axis, k):
    n = SIZES[axis]
    out = dict(c)
    out[axis] = rem(c[axis] + (k % n), n)
    return out


def dot_rows(a, b):
    return lax.dot_general(a, b, (((1,), (1,)), ((), ())), preferred_element_type=F32)


def dot_plain(a, b):
    return lax.dot_general(a, b, (((1,), (0,)), ((), ())), preferred_element_type=F32)


def dot_first(a, b):
    return lax.dot_general(a, b, (((0,), (0,)), ((), ())), preferred_element_type=F32)


def kernel(
    hid_in, q_in, k_in, v_in, g_in, doc_in, proj_in,
    outq_ref, outkv_ref,
    hid, q, g, kw, vw, docs, bias, pg, dq, dkv, acc, lr, left, dup, perm,
    zq, rq, xq, xr, yq, yr, wq, wr,
    zk, rk, ck, cr, xk, xkr, yk, ykr, kv_sum,
    relay, cb, cbr, db, dbr, qb, qbr, qc2, qcr,
    load_sem,
    by_send, by_recv, bqx_send, bqx_recv,
    bx_send, bx_recv, bz_send, bz_recv,
    rel_send, rel_recv,
    halo_send, halo_recv,
    gz_send, gz_recv, gy_send, gy_recv, gc_send, gc_recv,
    rc_send, rc_recv, qx_send, qx_recv, qy_send, qy_recv, qz_send, qz_recv,
    kz_send, kz_recv, kx_send, kx_recv, ky_send, ky_recv,
):
    c = here()
    s = lax.axis_index("seq")
    d = lax.axis_index("dp")
    core, x, y, z = c["core"], c["x"], c["y"], c["z"]
    y_lo = rem(y, 2)
    nxt = {"seq": rem(s + 1, 32), "dp": d}
    prv = {"seq": rem(s + 31, 32), "dp": d}
    sibling = device(moved(c, "core", 1))
    across = device(
        {"core": 1 - core, "x": rem(x + jnp.where(core == 1, 1, 3), 4), "y": y, "z": z}
    )
    turn = (x == 3) & (core == 1)
    over, back = device(moved(c, "y", 2)), device(moved(c, "y", -2))

    def zstep(k):
        return rem(z + jnp.where(core == 0, k + 8, 8 - k), 8)

    def zdev(k):
        n = dict(c)
        n["z"] = zstep(k)
        return device(n)

    barrier = pltpu.get_barrier_semaphore()
    peers = [nxt, prv, sibling, across]
    for axis in ("x", "y", "z"):
        for k in range(1, SIZES[axis]):
            peers.append(device(moved(c, axis, k)))
    for p in peers:
        pl.semaphore_signal(barrier, inc=1, device_id=p, device_id_type=MESH)

    loads = [
        pltpu.make_async_copy(doc_in, docs.at[0], load_sem.at[0]),
        pltpu.make_async_copy(k_in, kw.at[pl.ds(TOK, TOK)], load_sem.at[1]),
        pltpu.make_async_copy(v_in, vw.at[pl.ds(TOK, TOK)], load_sem.at[2]),
        pltpu.make_async_copy(q_in, q, load_sem.at[3]),
        pltpu.make_async_copy(g_in, g, load_sem.at[4]),
        pltpu.make_async_copy(
            proj_in, pg.at[pl.ds(pl.multiple_of(d * BLOCK, BLOCK), BLOCK)], load_sem.at[5]
        ),
        pltpu.make_async_copy(hid_in, hid, load_sem.at[6]),
    ]
    for cp in loads:
        cp.start()

    pl.semaphore_wait(barrier, len(peers))

    def remote(src, dst, send, recv, to):
        return pltpu.make_async_remote_copy(
            src_ref=src, dst_ref=dst, send_sem=send, recv_sem=recv, device_id=to, device_id_type=MESH
        )

    sent = []

    def go(cp):
        cp.start()
        sent.append(cp)
        return cp

    def prow(w, b, h, u=None):
        if u is None:
            return pg.at[pl.ds(pl.multiple_of((w * 2 + b) * BLOCK + h * HALF, HALF), HALF)]
        return pg.at[pl.ds(pl.multiple_of((w * 2 + b) * BLOCK + h * HALF + u * QUARTER, QUARTER), QUARTER)]

    def own_quarter(u):
        return proj_in.at[pl.ds(pl.multiple_of(core * HALF + u * QUARTER, QUARTER), QUARTER)]

    zf, zb = zdev(1), zdev(-1)
    yu, yd = device(moved(c, "y", 1)), device(moved(c, "y", -1))
    for u in range(2):
        go(remote(own_quarter(u), prow(z, y_lo, core, u), gz_send.at[u], gz_recv.at[u], zf))
        go(remote(own_quarter(u), prow(z, y_lo, core, u), gz_send.at[8 + u], gz_recv.at[8 + u], zb))
    def halo_copy(t, i, to, src=None):
        cols = pl.ds(i * PIECE, PIECE)
        slot = t * PIECES + i
        at = (kw, vw)[t].at[pl.ds(0, TOK), cols]
        return remote((k_in, v_in)[t].at[:, cols] if src is None else src, at, halo_send.at[slot], halo_recv.at[slot], to)

    def relay_copy(t, i):
        cols = pl.ds(i * PIECE, PIECE)
        slot = t * 2 + i - 2
        return remote((k_in, v_in)[t].at[:, cols], relay.at[slot], rel_send.at[slot], rel_recv.at[slot], over)

    def pass_on(t, i):
        return halo_copy(t, i, across, relay.at[t * 2 + i - 2])

    loads[0].wait()
    docs_copy = go(remote(docs.at[0], docs.at[1], halo_send.at[2 * PIECES], halo_recv.at[2 * PIECES], nxt))
    for i in range(2):
        for t in range(2):
            go(halo_copy(t, i, nxt))

    @pl.when(turn)
    def _():
        for i in (2, 3):
            for t in range(2):
                relay_copy(t, i).start()

    @pl.when(jnp.logical_not(turn))
    def _():
        for i in (2, 3):
            for t in range(2):
                halo_copy(t, i, nxt).start()

    def relay_pass(i):
        @pl.when(turn)
        def _():
            for t in range(2):
                relay_copy(t, i).wait_recv()
                pass_on(t, i).start()

    def halo_wait(i):
        for t in range(2):
            halo_copy(t, i, nxt).wait_recv()

    def halo_sent():
        @pl.when(turn)
        def _():
            for i in (2, 3):
                for t in range(2):
                    relay_copy(t, i).wait_send()
                    pass_on(t, i).wait_send()

        @pl.when(jnp.logical_not(turn))
        def _():
            for i in (2, 3):
                for t in range(2):
                    halo_copy(t, i, nxt).wait_send()

    ahead = [0, 1, -1, 2, -2, 3, -3, 4]

    def y_way(j, u):
        return j not in (0, 2) and (j % 2 == 1) == (u == 0)

    def y_send(j, u, src):
        ref = prow(zstep(-ahead[j]), y_lo, core, u)
        go(remote(src, ref, gy_send.at[2 * j + u], gy_recv.at[2 * j + u], yu if y_way(j, u) else yd))

    for u in range(2):
        y_send(0, u, own_quarter(u))

    def core_send(slot, w, b):
        ref = prow(w, b, core)
        go(remote(ref, ref, gc_send.at[slot], gc_recv.at[slot], sibling))

    def z_arrival(j, u):
        w = zstep(-ahead[j])
        ref = prow(w, y_lo, core, u)
        k = (j - 1) // 2
        slot = 2 * k + u if j % 2 else 8 + 2 * k + u
        remote(ref, ref, gz_send.at[slot], gz_recv.at[slot], zf).wait_recv()
        if j < 6:
            go(remote(ref, ref, gz_send.at[slot + 2], gz_recv.at[slot + 2], zf if j % 2 else zb))
        y_send(j, u, ref)
        if u:
            core_send(j - 1, w, y_lo)

    def y_arrival(j):
        w = zstep(-ahead[j])
        for u in range(2):
            ref = prow(w, 1 - y_lo, core, u)
            remote(ref, ref, gy_send.at[2 * j + u], gy_recv.at[2 * j + u], yu).wait_recv()
        core_send(7 + j, w, 1 - y_lo)

    def core_arrival(slot):
        w, b = (zstep(ahead[slot + 1]), y_lo) if slot < 7 else (zstep(ahead[slot - 7]), 1 - y_lo)
        ref = prow(w, b, 1 - core)
        remote(ref, ref, gc_send.at[slot], gc_recv.at[slot], sibling).wait_recv()

    def low_part(w, b, h):
        at = pl.multiple_of((w * 2 + b) * BLOCK + h * HALF, HALF)
        return dot_plain(hid[:, pl.ds(at, HALF)], pg[pl.ds(at, HALF)])

    def low_core(slot):
        w, b = (zstep(ahead[slot + 1]), y_lo) if slot < 7 else (zstep(ahead[slot - 7]), 1 - y_lo)
        return low_part(w, b, 1 - core)

    def add_low(parts):
        tot = parts[0]
        for p in parts[1:]:
            tot = tot + p
        acc[...] += tot

    score_scale = 1.0 / HD**0.5

    def attend(gi):
        wide = pl.multiple_of(gi * 512, 512)
        thin = pl.multiple_of(gi * HD, HD)
        qh = [q[:, pl.ds(wide + j * HD, HD)] for j in range(4)]
        gh = [g[:, pl.ds(wide + j * HD, HD)] for j in range(4)]
        q4 = jnp.concatenate(qh, axis=0)
        g4 = jnp.concatenate(gh, axis=0)
        kwin = kw[:, pl.ds(thin, HD)]
        vwin = vw[:, pl.ds(thin, HD)]
        sc = dot_rows(q4, kwin).reshape(4, TOK, 256) * score_scale + bias[...][None]
        sc = sc.reshape(512, 256)
        peak = jnp.max(sc, axis=1, keepdims=True)
        e = jnp.exp(sc - peak)
        att = e * (1.0 / jnp.sum(e, axis=1, keepdims=True))
        low = att.astype(BF)
        da = dot_rows(g4, vwin)
        delta = jnp.sum(low.astype(F32) * da, axis=1, keepdims=True)
        ds = (att * (da - delta)).astype(BF)
        dqv = (dot_plain(ds, kwin) * score_scale).astype(BF)
        for j in range(4):
            dq[:, pl.ds(wide + j * HD, HD)] = dqv[j * TOK : (j + 1) * TOK]
        dkv[pl.ds(0, 2 * TOK), pl.ds(thin, HD)] = (dot_first(ds, q4) * score_scale).astype(BF)
        dkv[pl.ds(2 * TOK, 2 * TOK), pl.ds(thin, HD)] = dot_first(low, g4).astype(BF)

    ri = lax.broadcasted_iota(jnp.int32, (512, RANK), 0)
    ci = lax.broadcasted_iota(jnp.int32, (512, RANK), 1)
    want = ((ri & 127) >> 3) * 16 + (ri >> 7) * 4 + (ri & 3)
    dup[...] = jnp.where(ci == want, 1.0, 0.0).astype(BF)
    ri = lax.broadcasted_iota(jnp.int32, (512, 512), 0)
    ci = lax.broadcasted_iota(jnp.int32, (512, 512), 1)
    want = ((ci & 127) >> 5) * 128 + (ci >> 7) * 32 + (ci & 31)
    perm[...] = jnp.where(ri == want, 1.0, 0.0).astype(BF)

    docs_copy.wait_recv()
    mine = jnp.broadcast_to(docs[0].astype(F32), (TOK, TOK))
    before = jnp.broadcast_to(docs[1].astype(F32), (TOK, TOK))
    before = jnp.where(s == 0, -1.0, before)
    rows = jnp.transpose(mine)
    causal = lax.broadcasted_iota(jnp.int32, (TOK, TOK), 1) <= lax.broadcasted_iota(jnp.int32, (TOK, TOK), 0)
    bias[:, TOK:] = jnp.where(causal & (mine == rows), 0.0, -jnp.inf)
    bias[:, :TOK] = jnp.where(before == rows, 0.0, -jnp.inf)

    for cp in loads[1:5]:
        cp.wait()
    z_arrival(1, 0)
    z_arrival(2, 0)
    halo_wait(0)
    attend(0)
    z_arrival(1, 1)
    z_arrival(2, 1)
    y_arrival(0)
    attend(1)
    relay_pass(2)
    z_arrival(3, 0)
    z_arrival(4, 0)
    halo_wait(1)
    attend(2)
    relay_pass(3)
    z_arrival(3, 1)
    z_arrival(4, 1)
    y_arrival(1)
    attend(3)
    z_arrival(5, 0)
    z_arrival(6, 0)
    y_arrival(2)
    halo_wait(2)
    attend(4)
    z_arrival(5, 1)
    z_arrival(6, 1)
    attend(5)
    z_arrival(7, 0)
    y_arrival(3)
    halo_wait(3)
    attend(6)
    z_arrival(7, 1)
    y_arrival(4)
    attend(7)
    y_arrival(5)
    loads[5].wait()
    loads[6].wait()
    at = pl.multiple_of(d * BLOCK, BLOCK)
    acc[...] = dot_plain(hid[:, pl.ds(at, BLOCK)], pg[pl.ds(at, BLOCK)])
    add_low([low_part(zstep(-ahead[j]), y_lo, core) for j in range(1, 8)])
    y_arrival(6)
    add_low([low_part(zstep(-ahead[j]), 1 - y_lo, core) for j in range(7)])
    y_arrival(7)
    order = [0, 1, 7, 2, 3, 8, 9, 4, 10, 11, 5, 6, 12, 13, 14]
    add_low([low_part(zstep(-ahead[7]), 1 - y_lo, core)])
    for some in (order[:9], order[9:13], order[13:]):
        for slot in some:
            core_arrival(slot)
        add_low([low_core(slot) for slot in some])

    lr[pl.ds(TOK, TOK)] = acc[...].astype(BF)
    lr_copy = go(
        remote(lr.at[pl.ds(TOK, TOK)], lr.at[pl.ds(0, TOK)], halo_send.at[2 * PIECES + 1], halo_recv.at[2 * PIECES + 1], nxt)
    )
    turned = jnp.transpose(acc[...]).astype(BF)

    def project(gi):
        part = dot_plain(turned, dq[:, pl.ds(pl.multiple_of(gi * 512, 512), 512)]).astype(BF)
        for j in range(4):
            piece = part[:, j * HD : (j + 1) * HD].reshape(8, 2, 16, HD)
            at_x = rem(2 * gi + j // 2, 4)
            for lo in range(2):
                zq[j % 2, at_x, (gi // 2) * 2 + lo] = piece[:, lo]

    def project_even(i, carry):
        project(2 * i)
        return carry

    def project_odd(i, carry):
        project(2 * i + 1)
        return carry

    lax.fori_loop(0, 4, project_even, 0)
    qc = [go(remote(zq.at[1 - core, pl.ds(0, 2)], rq.at[pl.ds(0, 2)], rc_send.at[0], rc_recv.at[0], sibling))]
    lax.fori_loop(0, 4, project_odd, 0)
    qc.append(go(remote(zq.at[1 - core, pl.ds(2, 2)], rq.at[pl.ds(2, 2)], rc_send.at[1], rc_recv.at[1], sibling)))

    lr_copy.wait_recv()
    spread = dot_rows(dup[...], lr[...])
    kind = (lax.broadcasted_iota(jnp.int32, (512, 256), 0) >> 2) & 1
    left[:, : 2 * TOK] = jnp.where(kind == 0, spread, 0.0).astype(BF)
    left[:, 2 * TOK :] = jnp.where(kind == 1, spread, 0.0).astype(BF)
    def qx_copy(at):
        slot = rem(at - x + 3, 4)
        to = device({"core": core, "x": at, "y": y, "z": z})
        part = (pl.ds(0, 8), pl.ds(0, FAR))
        return remote(xq.at[(at, *part)], xr.at[(slot, *part)], qx_send.at[slot], qx_recv.at[slot], to)

    def qx_start(at):
        if at % 2 == 0:
            qc[at // 2].wait_recv()
        both_cores = (zq[core, at].astype(F32) + rq[at].astype(F32)).astype(BF)
        xq[at, :, :FAR] = both_cores[:, :FAR]
        qb[:, at] = both_cores[:, FAR:]

        @pl.when(x != at)
        def _():
            qx_copy(at).start()

    def qx_wait(recv):
        for k in range(1, 4):
            cp = qx_copy(rem(x + k, 4))
            if recv:
                cp.wait_recv()
            else:
                cp.wait_send()

    kc = []
    for a in range(0, KVH, 2):
        both = dot_plain(left[...], dkv[:, a * HD : (a + 2) * HD]).astype(BF)
        for t in range(2):
            wide = jnp.concatenate(
                [both[i * 128 : (i + 1) * 128, t * HD : (t + 1) * HD] for i in range(4)], axis=1
            )
            wide = dot_plain(wide, perm[...]).astype(BF)
            for b in range(4):
                zk[b % 2, a // 2, :, t * 2 + b // 2] = wide[:, b * HD : (b + 1) * HD].reshape(8, 16, HD)
        yh = a // 2
        kc.append(go(remote(zk.at[1 - core, yh], rk.at[yh], rc_send.at[2 + yh], rc_recv.at[2 + yh], sibling)))
        if a < 4:
            qx_start(a)
            qx_start(a + 1)

    by = []
    for k in (4, 3, 5, 2, 6, 1, 7):
        at = rem(y + k, 8)
        by.append(go(remote(qb.at[at], qbr.at[k - 1], by_send.at[k - 1], by_recv.at[k - 1], device(moved(c, "y", k)))))
    for yh in range(2):
        kc[yh].wait_recv()
        ck[:, :, yh] = (zk[core, yh].astype(F32) + rk[yh].astype(F32)).astype(BF)
    kz = []
    for k in (4, 3, 5, 2, 6, 1, 7):
        at = rem(z + k, 8)
        kz.append(go(remote(ck.at[at], cr.at[k - 1], kz_send.at[k - 1], kz_recv.at[k - 1], device(moved(c, "z", k)))))
    for yh in range(2):
        kc[2 + yh].wait_recv()
        for at in range(4):
            cb[at, :, yh] = (zk[core, 2 + yh, :, at].astype(F32) + rk[2 + yh, :, at].astype(F32)).astype(BF)
    bx = []
    for k in (2, 1, 3):
        at = rem(x + k, 4)
        bx.append(go(remote(cb.at[at], cbr.at[k - 1], bx_send.at[k - 1], bx_recv.at[k - 1], device(moved(c, "x", k)))))

    qx_wait(True)
    qy = []
    for k in (4, 3, 5, 2, 6, 1, 7, 0):
        at = rem(y + k, 8)
        tot = xq[x, at, :FAR].astype(F32)
        for i in range(3):
            tot = tot + xr[i, at, :FAR].astype(F32)
        yq[at] = tot.astype(BF)
        if k:
            qy.append(go(remote(yq.at[at], yr.at[k - 1], qy_send.at[k - 1], qy_recv.at[k - 1], device(moved(c, "y", k)))))
    for cp in by:
        cp.wait_recv()
    bqx = []
    for k in (2, 1, 3, 0):
        at = rem(x + k, 4)
        tot = qb[y, at].astype(F32)
        for i in range(7):
            tot = tot + qbr[i, at].astype(F32)
        qc2[at] = tot.astype(BF)
        if k:
            bqx.append(go(remote(qc2.at[at], qcr.at[k - 1], bqx_send.at[k - 1], bqx_recv.at[k - 1], device(moved(c, "x", k)))))
    for cp in bx:
        cp.wait_recv()
    bz = []
    tot = cb[x].astype(F32)
    for i in range(3):
        tot = tot + cbr[i].astype(F32)
    db[...] = tot.astype(BF)
    for k in (4, 3, 5, 2, 6, 1, 7):
        at = rem(z + k, 8)
        bz.append(go(remote(db.at[at], dbr.at[k - 1], bz_send.at[k - 1], bz_recv.at[k - 1], device(moved(c, "z", k)))))
    for cp in kz:
        cp.wait_recv()
    kx = []
    for k in (2, 1, 3, 0):
        at = rem(x + k, 4)
        tot = ck[z, at].astype(F32)
        for i in range(7):
            tot = tot + cr[i, at].astype(F32)
        xk[at] = tot.astype(BF)
        if k:
            kx.append(go(remote(xk.at[at], xkr.at[k - 1], kx_send.at[k - 1], kx_recv.at[k - 1], device(moved(c, "x", k)))))
    for cp in qy:
        cp.wait_recv()
    tot = yq[y].astype(F32)
    for i in range(7):
        tot = tot + yr[i].astype(F32)
    wq[pl.ds(0, FAR)] = tot.astype(BF)
    for cp in bqx:
        cp.wait_recv()
    tot = qc2[x].astype(F32)
    for i in range(3):
        tot = tot + qcr[i].astype(F32)
    wq[pl.ds(FAR, 8 - FAR)] = tot.astype(BF)
    qz = []
    for k in (4, 3, 5, 2, 6, 1, 7):
        at = rem(z + k, 8)
        qz.append(go(remote(wq.at[at], wr.at[k - 1], qz_send.at[k - 1], qz_recv.at[k - 1], device(moved(c, "z", k)))))
    for cp in bz:
        cp.wait_recv()
    tot = db[z].astype(F32)
    for i in range(7):
        tot = tot + dbr[i].astype(F32)
    yk[pl.ds(2, 2)] = tot.astype(BF)
    for cp in kx:
        cp.wait_recv()
    tot = xk[x].astype(F32)
    for i in range(3):
        tot = tot + xkr[i].astype(F32)
    yk[pl.ds(0, 2)] = tot.astype(BF)
    ky = []
    for k in (4, 3, 5, 2, 6, 1, 7):
        to = moved(c, "y", k)
        ky.append(go(remote(yk.at[to["y"] // 2], ykr.at[k - 1], ky_send.at[k - 1], ky_recv.at[k - 1], device(to))))
    for cp in qz:
        cp.wait_recv()
    tot = wq[z].astype(F32)
    for i in range(7):
        tot = tot + wr[i].astype(F32)
    outq_ref[...] = tot
    for cp in ky:
        cp.wait_recv()
    tot = yk[y // 2].astype(F32)
    for i in range(7):
        tot = tot + ykr[i].astype(F32)
    kv_sum[...] = tot
    outkv_ref[...] = kv_sum[pl.ds(pl.multiple_of(y_lo * 8, 8), 8)]
    for cp in sent:
        cp.wait_send()
    halo_sent()
    qx_wait(False)


def reduced(hid, q, k, v, g, docs, proj):
    any_spec = pl.BlockSpec(memory_space=pltpu.HBM)
    vmem = pl.BlockSpec(memory_space=pltpu.VMEM)
    dma = pltpu.SemaphoreType.DMA
    halos = 2 * PIECES + 2
    scratch = [
        pltpu.VMEM((TOK, DEPTH), BF),
        pltpu.VMEM((TOK, QCOLS), BF),
        pltpu.VMEM((TOK, QCOLS), BF),
        pltpu.VMEM((2 * TOK, KCOLS), BF),
        pltpu.VMEM((2 * TOK, KCOLS), BF),
        pltpu.VMEM((2, 1, TOK), jnp.int32),
        pltpu.VMEM((TOK, 2 * TOK), F32),
        pltpu.VMEM((DEPTH, RANK), BF),
        pltpu.VMEM((TOK, QCOLS), BF),
        pltpu.VMEM((4 * TOK, KCOLS), BF),
        pltpu.VMEM((TOK, RANK), F32),
        pltpu.VMEM((2 * TOK, RANK), BF),
        pltpu.VMEM((512, 4 * TOK), BF),
        pltpu.VMEM((512, RANK), BF),
        pltpu.VMEM((512, 512), BF),
        pltpu.VMEM((2, 4, 8, 8, 16, HD), BF),
        pltpu.VMEM((4, 8, 8, 16, HD), BF),
        pltpu.VMEM((4, 8, 8, 16, HD), BF),
        pltpu.VMEM((3, 8, 8, 16, HD), BF),
        pltpu.VMEM((8, FAR, 16, HD), BF),
        pltpu.VMEM((7, FAR, 16, HD), BF),
        pltpu.VMEM((8, 16, HD), BF),
        pltpu.VMEM((7, 16, HD), BF),
        pltpu.VMEM((2, 4, 8, 4, 16, HD), BF),
        pltpu.VMEM((4, 8, 4, 16, HD), BF),
        pltpu.VMEM((8, 4, 2, 16, HD), BF),
        pltpu.VMEM((7, 4, 2, 16, HD), BF),
        pltpu.VMEM((4, 2, 16, HD), BF),
        pltpu.VMEM((3, 2, 16, HD), BF),
        pltpu.VMEM((4, 16, HD), BF),
        pltpu.VMEM((7, 16, HD), BF),
        pltpu.VMEM((16, HD), F32),
        pltpu.VMEM((4, TOK, PIECE), BF),
        pltpu.VMEM((4, 8, 2, 16, HD), BF),
        pltpu.VMEM((3, 8, 2, 16, HD), BF),
        pltpu.VMEM((8, 2, 16, HD), BF),
        pltpu.VMEM((7, 2, 16, HD), BF),
        pltpu.VMEM((8, 4, 8 - FAR, 16, HD), BF),
        pltpu.VMEM((7, 4, 8 - FAR, 16, HD), BF),
        pltpu.VMEM((4, 8 - FAR, 16, HD), BF),
        pltpu.VMEM((3, 8 - FAR, 16, HD), BF),
        dma((7,)),
    ]
    for n in (7, 3, 3, 7, 4, halos, 14, 16, 15, 6, 3, 7, 7, 7, 3, 7):
        scratch += [dma((n,)), dma((n,))]
    return pl.pallas_call(
        kernel,
        out_shape=(jax.ShapeDtypeStruct((16, HD), F32), jax.ShapeDtypeStruct((8, HD), F32)),
        in_specs=[any_spec] * 7,
        out_specs=(vmem, vmem),
        scratch_shapes=scratch,
        compiler_params=pltpu.CompilerParams(
            collective_id=0, has_side_effects=True, vmem_limit_bytes=62 * 1024 * 1024
        ),
        name="backward",
    )(hid, q, k, v, g, docs, proj)


def adam_update(first_moment, second_moment, gradient):
    first_new = beta_first * first_moment + (1.0 - beta_first) * gradient
    second_new = beta_second * second_moment + (1.0 - beta_second) * gradient * gradient
    corrected_first = first_new / (1.0 - beta_first**ADAM_STEP)
    corrected_second = second_new / (1.0 - beta_second**ADAM_STEP)
    return (first_new, second_new, corrected_first / (jnp.sqrt(corrected_second) + adam_epsilon))


def on_device(
    hidden_in, queries, keys, values, out_grad, doc_ids, projection, mom1_q, mom2_q, mom1_kv, mom2_kv
):
    grad_q, grad_kv = reduced(
        hidden_in[0], queries[0], keys[0], values[0], out_grad[0], doc_ids, projection
    )
    grad_kv = grad_kv.reshape(2, 4, 4, 32).transpose(0, 2, 1, 3).reshape(2, 16, 32)
    return adam_update(mom1_q, mom2_q, grad_q) + adam_update(mom1_kv, mom2_kv, grad_kv)


def solution(mesh):
    in_specs = (
        P("dp", "seq", None),
        P("dp", "seq", None),
        P("dp", "seq", None),
        P("dp", "seq", None),
        P("dp", "seq", None),
        P("dp", "seq"),
        P("dp", None),
        P("dp", "seq"),
        P("dp", "seq"),
        P(None, "dp", "seq"),
        P(None, "dp", "seq"),
    )
    out_specs = (
        P("dp", "seq"),
        P("dp", "seq"),
        P("dp", "seq"),
        P(None, "dp", "seq"),
        P(None, "dp", "seq"),
        P(None, "dp", "seq"),
    )
    return jax.shard_map(
        on_device, mesh=mesh, in_specs=in_specs, out_specs=out_specs, check_vma=False
    )
```
